32 devices in a mesh: dp: 8 (over y, x, core), seq: 4 (over z).
Axes of the slice: x: 2, y: 2, z: 4, core: 2. Of those that a mesh axis runs over, the one named last changes fastest.
Arguments:
- projections: bfloat16 [8192, 3584], P(('dp', 'seq')), may hold values from -80 to 80
- grad_out: bfloat16 [8192, 2560], P(('dp', 'seq')), may hold values from -6 to 6
- bias_q: bfloat16 [2560], replicated, may hold values from -3 to 3
- half_kind: int32 [8, 2], replicated, may hold values from 0 to 1, as said below
- dest_half: int32 [8, 2], replicated, may hold values from 0 to 15, as said below
Outputs:
- grad_projections: bfloat16 [8192, 3584], P(('dp', 'seq'))
- bias_grad: float32 [2560], P(('dp', 'seq'))
- value_bias_grad: float32 [512], P(('dp', 'seq'))
The draws below stay inside these ranges and needn't reach their ends.
Inputs may be any that keep to these rules, and one draw needn't show every extreme that they name: `half_kind`: 0: the half is one document; 1: it is two documents of a quarter window each. A permutation of the 16 halves: source half (w, h) goes to destination window dest_half // 2, half dest_half % 2.
All inputs are finite; a program needn't handle non-finite values.
Results may differ from the reference program's by a relative error of at most 0.0063.
Values may be sent and summed in bfloat16 or wider, within the bound.
No kernel may reach another device: no remote copies, remote signals or barrier semaphores. Data moves between devices by JAX's collectives and lax.ppermute only.
A program may use at most 128 MiB of HBM per device.

```python
import math
import jax
import jax.numpy as jnp
from jax import lax

QH = 20
KVH = 4
HEAD = 128
NWIN = 8
TOKENS = 8192
QKVF = 3584


def plan_tables(key):
    half_kinds = jax.random.randint(jax.random.fold_in(key, 11), (2 * NWIN,), 0, 2).astype(jnp.int32)
    order_key = jax.random.permutation(jax.random.fold_in(key, 12), 2 * NWIN).astype(jnp.int32)
    ranking = jnp.argsort(half_kinds * (2 * NWIN) + order_key, stable=True)
    flip_bits = jax.random.randint(jax.random.fold_in(key, 13), (NWIN,), 0, 2).astype(jnp.int32)
    places = jnp.arange(2 * NWIN, dtype=jnp.int32)
    windows = places % NWIN
    side_bits = (places // NWIN + flip_bits[windows]) % 2
    destination = jnp.zeros((2 * NWIN,), jnp.int32).at[ranking].set(windows * 2 + side_bits)
    return (half_kinds.reshape(NWIN, 2), destination.reshape(NWIN, 2))


def draw_half_kind(key, part):
    shared = plan_tables(key)
    return shared[0]


def draw_dest_half(key, part):
    shared = plan_tables(key)
    return shared[1]


def draw_projections(key, part):
    key = jax.random.fold_in(key, 3)
    whole = jnp.clip(jax.random.normal(jax.random.fold_in(key, 1), (TOKENS, QKVF), jnp.float32), -6.0, 6.0)
    return whole.astype(jnp.bfloat16)


def block_scale(stream_key, shape, shards, smallest, largest):
    def one(dim, shards_of):
        heights = jax.random.uniform(jax.random.fold_in(jax.random.fold_in(stream_key, 6), dim), (shards_of,), jnp.float32, smallest / len(shards), largest / len(shards))
        return jnp.repeat(jnp.exp(heights), shape[dim] // shards_of).reshape((-1,) + (1,) * (len(shape) - dim - 1))

    loudness = one(*shards[0])
    for cut in shards[1:]:
        loudness = loudness * one(*cut)
    return loudness


def bell_draw(stream_key, shape, spread, most, split=(), kind=jnp.bfloat16):
    values = spread * jax.random.normal(stream_key, shape, jnp.float32)
    if split:
        values = values * block_scale(stream_key, shape, split, -0.22, 0.18)
    return jnp.clip(values, -most, most).astype(kind)


def setup_inputs(seed: int = 0) -> dict:
    arg_keys = jax.random.split(jax.random.key(seed), 6)
    projections = draw_projections(jax.random.fold_in(arg_keys[5], 71), 0)
    grad_out = bell_draw(arg_keys[1], (TOKENS, QH * HEAD), 1.0, 6.0, ((0, 32),))
    bias_q = bell_draw(arg_keys[2], (QH * HEAD,), 0.5, 3.0)
    half_kind = draw_half_kind(jax.random.fold_in(arg_keys[5], 71), 0)
    dest_half = draw_dest_half(jax.random.fold_in(arg_keys[5], 71), 0)
    return {"projections": projections, "grad_out": grad_out, "bias_q": bias_q, "half_kind": half_kind, "dest_half": dest_half}


NEG = -1e+30

def settle(values):
    return lax.optimization_barrier(values.astype(jnp.bfloat16)).astype(jnp.float32)

def half_grads(block_rows, block_grad, kind_here, bias_q):
    length = block_rows.shape[0]
    q_width = QH * HEAD
    kv_width = KVH * HEAD
    group_size = QH // KVH
    queries = settle(block_rows[:, :q_width].astype(jnp.float32) + bias_q.astype(jnp.float32))
    queries = queries.reshape(length, KVH, group_size, HEAD)
    key_rows = block_rows[:, q_width:q_width + kv_width].astype(jnp.float32).reshape(length, KVH, HEAD)
    value_rows = block_rows[:, q_width + kv_width:].astype(jnp.float32).reshape(length, KVH, HEAD)
    grad_rows = block_grad.astype(jnp.float32).reshape(length, KVH, group_size, HEAD)
    offsets = jnp.arange(length, dtype=jnp.int32)
    documents = kind_here * (offsets // (length // 2))
    allowed = (documents[:, None] == documents[None, :]) & (offsets[None, :] <= offsets[:, None])
    score_scale = 1.0 / math.sqrt(HEAD)
    scores = jnp.einsum('qkge,tke->kgqt', queries, key_rows) * score_scale
    scores = jnp.where(allowed, scores, NEG)
    row_max = lax.optimization_barrier(jnp.max(scores, axis=-1, keepdims=True))
    exp_rows = jnp.exp(scores - row_max)
    prob_rows = exp_rows / lax.optimization_barrier(jnp.sum(exp_rows, axis=-1, keepdims=True))
    grad_prob = jnp.einsum('qkge,tke->kgqt', grad_rows, value_rows)
    row_delta = lax.optimization_barrier(jnp.sum(prob_rows * grad_prob, axis=-1, keepdims=True))
    grad_score = settle(prob_rows * (grad_prob - row_delta) * score_scale)
    weights = settle(prob_rows)
    grad_query = jnp.einsum('kgqt,tke->qkge', grad_score, key_rows).reshape(length, q_width)
    grad_key = jnp.einsum('kgqt,qkge->tke', grad_score, queries).reshape(length, kv_width)
    grad_value = jnp.einsum('kgqt,qkge->tke', weights, grad_rows).reshape(length, kv_width)
    grad_rows_out = jnp.concatenate([grad_query, grad_key, grad_value], axis=1).astype(jnp.bfloat16)
    return (grad_rows_out, lax.optimization_barrier(jnp.sum(grad_query, axis=0)), lax.optimization_barrier(jnp.sum(grad_value, axis=0)))

def reference(projections, grad_out, bias_q, half_kind, dest_half):
    half_count = 2 * NWIN
    half_rows = TOKENS // half_count
    source_half = jnp.argsort(dest_half.reshape(-1)).astype(jnp.int32)
    half_kinds = half_kind.reshape(-1)[source_half]
    packed_projections = projections.reshape(half_count, half_rows, QKVF)[source_half]
    packed_grad = grad_out.reshape(half_count, half_rows, QH * HEAD)[source_half]

    def one_half(half_items):
        return half_grads(half_items[0], half_items[1], half_items[2], bias_q)
    grad_halves, query_sums, value_sums = lax.map(one_half, (packed_projections, packed_grad, half_kinds))
    grad_projections = grad_halves.reshape(TOKENS, QKVF)
    factor = 1.0 / math.sqrt(TOKENS)
    bias_grad = lax.optimization_barrier(jnp.sum(query_sums, axis=0)) * factor
    value_bias_grad = lax.optimization_barrier(jnp.sum(value_sums, axis=0)) * factor
    return (grad_projections, bias_grad, value_bias_grad)
```

```python
import math
from functools import partial

import jax
import jax.numpy as jnp
from jax import lax
from jax.experimental import pallas as pl
from jax.experimental.pallas import tpu as pltpu
from jax.sharding import PartitionSpec as P

HEAD = 128
NEG = -1e30
F32 = jnp.float32
BF16 = jnp.bfloat16
SCALE = 1.0 / math.sqrt(HEAD)


def dot(a, b, a_dim, b_dim):
    return lax.dot_general(a, b, (((a_dim,), (b_dim,)), ((), ())), preferred_element_type=F32)


def attention_kernel(
    group_size, earlier, seen_ref, q_ref, k_ref, v_ref, grad_ref, bias_ref, *refs
):
    k_off_ref, v_off_ref = refs[:2] if earlier else (None, None)
    outs = refs[2:] if earlier else refs
    dq_ref, dkv_ref, q_sum_ref, v_sum_ref = outs[:4]
    off_ref = outs[4] if earlier else None
    rows = q_ref.shape[0]

    def grads(seen):
        keys = [k_ref[...]] + [k_off_ref[d] for d in range(seen)]
        values = [v_ref[...]] + [v_off_ref[d] for d in range(seen)]
        key_at = lax.broadcasted_iota(jnp.int32, (rows, rows), 0)
        query_at = lax.broadcasted_iota(jnp.int32, (rows, rows), 1)
        causal = key_at <= query_at
        grad_keys = [jnp.zeros((rows, HEAD), F32) for _ in keys]
        grad_values = [jnp.zeros((rows, HEAD), F32) for _ in keys]
        for head in range(group_size):
            cols = slice(head * HEAD, (head + 1) * HEAD)
            query = (q_ref[:, cols].astype(F32) + bias_ref[:, cols].astype(F32)).astype(BF16)
            grad = grad_ref[:, cols]
            scores = [dot(key, query, 1, 1) for key in keys]
            scores[0] = jnp.where(causal, scores[0], NEG)
            top = jnp.max(scores[0], axis=0, keepdims=True)
            for other in scores[1:]:
                top = jnp.maximum(top, jnp.max(other, axis=0, keepdims=True))
            exps = [jnp.exp((s - top) * SCALE) for s in scores]
            grad_probs = [dot(value, grad, 1, 1) for value in values]
            total = sum(jnp.sum(e, axis=0, keepdims=True) for e in exps)
            mixed = sum(
                jnp.sum(e * g, axis=0, keepdims=True) for e, g in zip(exps, grad_probs)
            )
            inverse = 1.0 / total
            delta = mixed * inverse
            scaled = inverse * SCALE
            grad_query = None
            for i, (e, g) in enumerate(zip(exps, grad_probs)):
                weights = (e * inverse).astype(BF16)
                grad_scores = (e * scaled * (g - delta)).astype(BF16)
                grad_values[i] = grad_values[i] + dot(weights, grad, 1, 0)
                grad_keys[i] = grad_keys[i] + dot(grad_scores, query, 1, 0)
                term = dot(grad_scores, keys[i], 0, 0)
                grad_query = term if grad_query is None else grad_query + term
            dq_ref[:, cols] = grad_query.astype(BF16)
            q_sum_ref[:, cols] = jnp.sum(grad_query, axis=0, keepdims=True)
        dkv_ref[0] = grad_keys[0]
        dkv_ref[1] = grad_values[0]
        v_sum = jnp.sum(grad_values[0], axis=0, keepdims=True)
        for i in range(earlier):
            if i < seen:
                off_ref[i, 0] = grad_keys[i + 1].astype(BF16)
                off_ref[i, 1] = grad_values[i + 1].astype(BF16)
                v_sum = v_sum + jnp.sum(grad_values[i + 1], axis=0, keepdims=True)
            else:
                off_ref[i] = jnp.zeros(off_ref.shape[1:], BF16)
        v_sum_ref[...] = v_sum

    for seen in range(earlier + 1):
        pl.when(seen_ref[0] == seen)(partial(grads, seen))


def attention(seen, projections, grad_out, bias, k_off, first, groups, q_width):
    rows, width = projections.shape
    kv_width = (width - q_width) // 2
    group_size = q_width // kv_width
    earlier = k_off.shape[0]
    wide = group_size * HEAD
    k_at = q_width // HEAD + first
    v_at = k_at + kv_width // HEAD
    in_specs = [
        pl.BlockSpec((rows, wide), lambda g, s: (0, first + g)),
        pl.BlockSpec((rows, HEAD), lambda g, s: (0, k_at + g)),
        pl.BlockSpec((rows, HEAD), lambda g, s: (0, v_at + g)),
        pl.BlockSpec((rows, wide), lambda g, s: (0, first + g)),
        pl.BlockSpec((1, wide), lambda g, s: (0, first + g)),
    ]
    operands = [projections, projections, projections, grad_out, bias]
    if earlier:
        in_specs += [
            pl.BlockSpec((earlier, None, rows, HEAD), lambda g, s: (0, 0, 0, g)),
            pl.BlockSpec((earlier, None, rows, HEAD), lambda g, s: (0, 1, 0, g)),
        ]
        operands += [k_off, k_off]
    out_specs = [
        pl.BlockSpec((rows, wide), lambda g, s: (0, g)),
        pl.BlockSpec((2, rows, HEAD), lambda g, s: (0, 0, g)),
        pl.BlockSpec((1, wide), lambda g, s: (0, g)),
        pl.BlockSpec((1, HEAD), lambda g, s: (0, g)),
    ]
    out_shape = [
        jax.ShapeDtypeStruct((rows, groups * wide), BF16),
        jax.ShapeDtypeStruct((2, rows, groups * HEAD), F32),
        jax.ShapeDtypeStruct((1, groups * wide), F32),
        jax.ShapeDtypeStruct((1, groups * HEAD), F32),
    ]
    if earlier:
        out_specs.append(pl.BlockSpec((earlier, 2, rows, HEAD), lambda g, s: (0, 0, 0, g)))
        out_shape.append(jax.ShapeDtypeStruct((earlier, 2, rows, groups * HEAD), BF16))
    flops = 10 * groups * group_size * rows * rows * HEAD * (1 + earlier)
    outs = pl.pallas_call(
        partial(attention_kernel, group_size, earlier),
        grid_spec=pltpu.PrefetchScalarGridSpec(
            num_scalar_prefetch=1, grid=(groups,), in_specs=in_specs, out_specs=out_specs
        ),
        out_shape=out_shape,
        compiler_params=pltpu.CompilerParams(vmem_limit_bytes=24 * 1024 * 1024),
        cost_estimate=pl.CostEstimate(
            flops=flops,
            bytes_accessed=4 * rows * groups * wide,
            transcendentals=groups * group_size * rows * rows * (1 + earlier),
        ),
        name="attention_grads",
    )(seen, *operands)
    return outs if earlier else (*outs, None)


def move_kernel(count, places_ref, *refs):
    sources, out_ref = refs[:-1], refs[-1]
    for i in range(count):
        for at, source in enumerate(sources):

            @pl.when(places_ref[0, i] == at)
            def _():
                out_ref[i] = source[places_ref[1, i]]


def moved(places, count, *sources):
    vmem = pl.BlockSpec(memory_space=pltpu.VMEM)
    return pl.pallas_call(
        partial(move_kernel, count),
        in_specs=[pl.BlockSpec(memory_space=pltpu.SMEM)] + [vmem for _ in sources],
        out_specs=vmem,
        out_shape=jax.ShapeDtypeStruct((count, *sources[0].shape[1:]), sources[0].dtype),
        compiler_params=pltpu.CompilerParams(vmem_limit_bytes=16 * 1024 * 1024),
        name="move_slices",
    )(places, *sources)


def plan(dest_half, seq_count):
    windows = dest_half.shape[0]
    ids = jnp.arange(windows, dtype=jnp.int32)
    side = lax.axis_index("seq") // (seq_count // 2)
    crosses = (dest_half % 2) != jnp.arange(2, dtype=jnp.int32)[None, :]
    rank = jnp.sum(
        jnp.where((ids[None, :] < ids[:, None])[:, :, None], crosses[None, :, :], False), axis=1
    ).astype(jnp.int32)
    count = jnp.sum(crosses[:, 0].astype(jnp.int32))
    mine = jnp.arange(2, dtype=jnp.int32) == side
    cross_here = jnp.any(crosses & mine[None, :], axis=1)
    rank_here = jnp.sum(jnp.where(mine[None, :], rank, 0), axis=1)
    sent = jnp.sum(
        jnp.where((rank_here[None, :] == ids[:, None]) & cross_here[None, :], ids[None, :], 0),
        axis=1,
    )
    hit = dest_half[None, :, :] == (2 * ids + side)[:, None, None]
    from_other = jnp.any(hit & crosses[None], axis=(1, 2)).astype(jnp.int32)
    place = jnp.sum(
        jnp.where(hit, jnp.where(crosses, rank, ids[:, None])[None], 0), axis=(1, 2)
    )
    return count, jnp.stack([jnp.zeros_like(sent), sent]), jnp.stack([from_other, place])


def local(projections, grad_out, bias_q, half_kind, dest_half):
    dp_count = lax.axis_size("dp")
    seq_count = lax.axis_size("seq")
    dp_at = lax.axis_index("dp")
    seq_at = lax.axis_index("seq")
    rows, width = projections.shape
    q_width = bias_q.shape[0]
    kv_width = (width - q_width) // 2
    span = seq_count // 2
    piece = seq_at % span
    kind = lax.dynamic_slice(half_kind, (dp_at, seq_at // span), (1, 1))[0, 0]
    seen = jnp.where(kind == 0, piece, piece % (span // 2)).reshape(1)

    def later(by):
        return [(i, i + by) for i in range(seq_count) if i // span == (i + by) // span]

    own_kv = projections[:, q_width:].reshape(rows, 2, kv_width).transpose(1, 0, 2)
    kv_off = jnp.stack([lax.ppermute(own_kv, "seq", later(d)) for d in range(1, span)])
    bias = bias_q.reshape(1, q_width)
    grad_query, own, q_sum, v_sum, off = attention(
        seen, projections, grad_out, bias, kv_off, 0, kv_width // HEAD, q_width
    )
    for d in range(1, span):
        back = [(b, a) for a, b in later(d)]
        own = own + lax.ppermute(off[d - 1], "seq", back).astype(F32)
    grad_kv = own.astype(BF16).transpose(1, 0, 2).reshape(rows, 2 * kv_width)
    total_rows = rows * dp_count * seq_count
    factor = 1.0 / math.sqrt(total_rows)
    devices = dp_count * seq_count
    terms = jnp.concatenate(
        [q_sum.reshape(devices, -1), v_sum.reshape(devices, -1)], axis=1
    )
    terms = jnp.sum(
        lax.all_to_all(terms, ("dp", "seq"), split_axis=0, concat_axis=0, tiled=True), axis=0
    )
    terms = terms * factor
    bias_grad = terms[: q_width // devices]
    value_bias_grad = terms[q_width // devices :]

    crossing, sends, places = plan(dest_half, seq_count)
    swap = [(i, (i + span) % seq_count) for i in range(seq_count)]
    whole = jnp.concatenate([grad_query, grad_kv], axis=1)
    spread = lax.all_to_all(
        whole.reshape(dp_count, rows // dp_count, width), "dp", split_axis=0, concat_axis=0, tiled=True
    )

    def across(count, spread):
        if count == 0:
            return spread
        sent = moved(sends, count, spread)
        got = lax.ppermute(sent, "seq", swap)
        return moved(places, dp_count, spread, got)

    step = max(1, dp_count // 8)
    levels = list(range(0, dp_count + 1, step))
    level = (crossing + step - 1) // step
    packed = lax.switch(level, [partial(across, n) for n in levels], spread)
    placed = lax.all_to_all(packed, "dp", split_axis=0, concat_axis=0, tiled=True)
    return (placed.reshape(rows, width), bias_grad, value_bias_grad)


def solution(mesh):
    in_specs = (P(("dp", "seq"), None), P(("dp", "seq"), None), P(), P(), P())
    out_specs = (P(("dp", "seq"), None), P(("dp", "seq")), P(("dp", "seq")))
    return jax.shard_map(local, mesh=mesh, in_specs=in_specs, out_specs=out_specs, check_vma=False)
```

```python
import math
from functools import partial, reduce

import jax
import jax.numpy as jnp
from jax import lax
from jax.experimental import pallas as pl
from jax.experimental.pallas import tpu as pltpu
from jax.sharding import PartitionSpec as P

HEAD = 128
NEG = -1e30
F32 = jnp.float32
BF16 = jnp.bfloat16
SCALE = 1.0 / math.sqrt(HEAD)


def dot(a, b, a_dim, b_dim):
    return lax.dot_general(a, b, (((a_dim,), (b_dim,)), ((), ())), preferred_element_type=F32)


def attention_kernel(
    group_size, earlier, at_ref, q_ref, k_ref, v_ref, grad_ref, bias_ref, *refs
):
    kv_off_ref = refs[0] if earlier else None
    outs = refs[1:] if earlier else refs
    dq_ref, dq_other_ref, dkv_ref, q_sum_ref, v_sum_ref = outs[:5]
    off_ref = outs[5] if earlier else None
    rows = q_ref.shape[0]

    keys = [k_ref[...]] + [kv_off_ref[d, 0] for d in range(earlier)]
    values = [v_ref[...]] + [kv_off_ref[d, 1] for d in range(earlier)]
    key_at = lax.broadcasted_iota(jnp.int32, (rows, rows), 0)
    query_at = lax.broadcasted_iota(jnp.int32, (rows, rows), 1)
    allowed = [key_at <= query_at] + [at_ref[0] > d for d in range(earlier)]

    def one_head(head, sums):
        grad_keys, grad_values = sums
        cols = slice(head * HEAD, (head + 1) * HEAD)
        query = (q_ref[:, cols].astype(F32) + bias_ref[:, cols].astype(F32)).astype(BF16)
        grad = grad_ref[:, cols]
        scores = [jnp.where(ok, dot(key, query, 1, 1), NEG) for ok, key in zip(allowed, keys)]
        tops = [jnp.max(s, axis=0, keepdims=True) for s in scores]
        top = reduce(jnp.maximum, tops)
        exps = [jnp.exp((s - top) * SCALE) for s in scores]
        grad_probs = [dot(value, grad, 1, 1) for value in values]
        total = sum(jnp.sum(e, axis=0, keepdims=True) for e in exps)
        mixed = sum(jnp.sum(e * g, axis=0, keepdims=True) for e, g in zip(exps, grad_probs))
        inverse = 1.0 / total
        delta = mixed * inverse
        scaled = inverse * SCALE
        weights = [(e * inverse).astype(BF16) for e in exps]
        grad_scores = [(e * scaled * (g - delta)).astype(BF16) for e, g in zip(exps, grad_probs)]
        grad_values = [t + dot(w, grad, 1, 0) for t, w in zip(grad_values, weights)]
        grad_keys = [t + dot(s, query, 1, 0) for t, s in zip(grad_keys, grad_scores)]
        grad_query = sum(dot(s, key, 0, 0) for s, key in zip(grad_scores, keys))
        rounded = grad_query.astype(BF16)
        first, second = rounded[: rows // 2], rounded[rows // 2 :]
        dq_ref[:, cols] = jnp.where(at_ref[1] == 0, first, second)
        dq_other_ref[:, cols] = jnp.where(at_ref[1] == 0, second, first)
        q_sum_ref[:, cols] = jnp.sum(grad_query, axis=0, keepdims=True)
        return grad_keys, grad_values

    zeros = [jnp.zeros((rows, HEAD), F32) for _ in keys]
    sums = (zeros, zeros)
    for head in range(group_size):
        sums = one_head(head, sums)
    grad_keys, grad_values = sums
    dkv_ref[0] = grad_keys[0]
    dkv_ref[1] = grad_values[0]
    v_sum_ref[...] = sum(jnp.sum(g, axis=0, keepdims=True) for g in grad_values)
    for d in range(earlier):
        off_ref[d, 0] = grad_keys[d + 1].astype(BF16)
        off_ref[d, 1] = grad_values[d + 1].astype(BF16)


def attention(at, projections, grad_out, bias, kv_off, first, groups, q_width, vmem):
    rows, width = projections.shape
    kv_width = (width - q_width) // 2
    group_size = q_width // kv_width
    earlier = kv_off.shape[0]
    wide = group_size * HEAD
    k_at = q_width // HEAD + first
    v_at = k_at + kv_width // HEAD
    in_specs = [
        pl.BlockSpec((rows, wide), lambda g, s: (0, first + g)),
        pl.BlockSpec((rows, HEAD), lambda g, s: (0, k_at + g)),
        pl.BlockSpec((rows, HEAD), lambda g, s: (0, v_at + g)),
        pl.BlockSpec((rows, wide), lambda g, s: (0, first + g)),
        pl.BlockSpec((1, wide), lambda g, s: (0, first + g)),
    ]
    operands = [projections, projections, projections, grad_out, bias]
    if earlier:
        in_specs.append(pl.BlockSpec((earlier, 2, rows, HEAD), lambda g, s: (0, 0, 0, g)))
        operands.append(kv_off)
    out_specs = [
        pl.BlockSpec((rows // 2, wide), lambda g, s: (0, g)),
        pl.BlockSpec((rows // 2, wide), lambda g, s: (0, g)),
        pl.BlockSpec((2, rows, HEAD), lambda g, s: (0, 0, g)),
        pl.BlockSpec((1, wide), lambda g, s: (0, g)),
        pl.BlockSpec((1, HEAD), lambda g, s: (0, g)),
    ]
    out_shape = [
        jax.ShapeDtypeStruct((rows // 2, groups * wide), BF16),
        jax.ShapeDtypeStruct((rows // 2, groups * wide), BF16),
        jax.ShapeDtypeStruct((2, rows, groups * HEAD), F32),
        jax.ShapeDtypeStruct((1, groups * wide), F32),
        jax.ShapeDtypeStruct((1, groups * HEAD), F32),
    ]
    if earlier:
        out_specs.append(pl.BlockSpec((earlier, 2, rows, HEAD), lambda g, s: (0, 0, 0, g)))
        out_shape.append(jax.ShapeDtypeStruct((earlier, 2, rows, groups * HEAD), BF16))
    flops = 10 * groups * group_size * rows * rows * HEAD * (1 + earlier)
    outs = pl.pallas_call(
        partial(attention_kernel, group_size, earlier),
        grid_spec=pltpu.PrefetchScalarGridSpec(
            num_scalar_prefetch=1, grid=(groups,), in_specs=in_specs, out_specs=out_specs
        ),
        out_shape=out_shape,
        compiler_params=pltpu.CompilerParams(vmem_limit_bytes=vmem * 1024 * 1024),
        cost_estimate=pl.CostEstimate(
            flops=flops,
            bytes_accessed=4 * rows * groups * wide,
            transcendentals=groups * group_size * rows * rows * (1 + earlier),
        ),
        name="attention_grads",
    )(at, *operands)
    return outs if earlier else (*outs, None)


def move_kernel(shape, far, places_ref, *refs):
    *refs, sem = refs
    sources, outs = refs[: len(refs) - len(shape)], refs[len(refs) - len(shape) :]
    first = 0
    for out_ref, count in zip(outs, shape):

        def fill(j, _, out_ref=out_ref, first=first):
            for at, source in enumerate(sources):

                @pl.when(places_ref[0, first + j] == at)
                def _():
                    if at < len(sources) - far:
                        out_ref[j] = source[places_ref[1, first + j]]
                    else:
                        copy = pltpu.make_async_copy(
                            source.at[places_ref[1, first + j]], out_ref.at[j], sem
                        )
                        copy.start()
                        copy.wait()

            return 0

        lax.fori_loop(0, count, fill, 0)
        first += count


def moved(places, shape, sources, far=0):
    vmem = pl.BlockSpec(memory_space=pltpu.VMEM)
    where = [vmem] * (len(sources) - far) + [pl.BlockSpec(memory_space=pl.ANY)] * far
    slice_shape = sources[0].shape[1:]
    return pl.pallas_call(
        partial(move_kernel, shape, far),
        in_specs=[pl.BlockSpec(memory_space=pltpu.SMEM)] + where,
        out_specs=[vmem for _ in shape],
        out_shape=[jax.ShapeDtypeStruct((n, *slice_shape), sources[0].dtype) for n in shape],
        scratch_shapes=[pltpu.SemaphoreType.DMA],
        compiler_params=pltpu.CompilerParams(vmem_limit_bytes=10 * 1024 * 1024),
        cost_estimate=pl.CostEstimate(flops=1, bytes_accessed=1, transcendentals=0),
        name="move_slices",
    )(places, *sources)


def pad_kernel(count, *refs):
    gots, outs = refs[: len(refs) // 2], refs[len(refs) // 2 :]
    for got, out in zip(gots, outs):
        out[:count] = got[...]


def padded(size, shapes, gots):
    count = gots[0].shape[0] if gots else 0
    vmem = pl.BlockSpec(memory_space=pltpu.VMEM)
    free = pl.BlockSpec(memory_space=pl.ANY)
    return pl.pallas_call(
        partial(pad_kernel, count) if gots else lambda *outs: None,
        in_specs=[vmem for _ in gots],
        out_specs=[vmem if gots else free for _ in shapes],
        out_shape=[jax.ShapeDtypeStruct((size, *shape), BF16) for shape in shapes],
        compiler_params=pltpu.CompilerParams(vmem_limit_bytes=10 * 1024 * 1024),
        name="pad_slices",
    )(*gots)


def join_kernel(widths, places_ref, *refs):
    out_ref = refs[-1]
    each = (len(refs) - 1) // len(widths)

    def fill(i, _):
        for at in range(each):

            @pl.when(places_ref[0, i] == at)
            def _():
                column = 0
                for chunk, wide in enumerate(widths):
                    source = refs[chunk * each + at]
                    out_ref[i, :, column : column + wide] = source[places_ref[1, i]]
                    column += wide

        return 0

    lax.fori_loop(0, out_ref.shape[0], fill, 0)


def joined(places, chunks):
    vmem = pl.BlockSpec(memory_space=pltpu.VMEM)
    widths = [sources[0].shape[-1] for sources in chunks]
    count, rows = places.shape[1], chunks[0][0].shape[1]
    return pl.pallas_call(
        partial(join_kernel, widths),
        in_specs=[pl.BlockSpec(memory_space=pltpu.SMEM)] + [vmem for c in chunks for _ in c],
        out_specs=vmem,
        out_shape=jax.ShapeDtypeStruct((count, rows, sum(widths)), BF16),
        compiler_params=pltpu.CompilerParams(vmem_limit_bytes=10 * 1024 * 1024),
        cost_estimate=pl.CostEstimate(flops=1, bytes_accessed=1, transcendentals=0),
        name="join_chunks",
    )(places, *[source for sources in chunks for source in sources])


def plan(dest_half, seq_count):
    windows = dest_half.shape[0]
    ids = jnp.arange(windows, dtype=jnp.int32)
    side = lax.axis_index("seq") // (seq_count // 2)
    crosses = (dest_half % 2) != jnp.arange(2, dtype=jnp.int32)[None, :]
    rank = jnp.sum(
        jnp.where((ids[None, :] < ids[:, None])[:, :, None], crosses[None, :, :], False), axis=1
    ).astype(jnp.int32)
    mine = jnp.arange(2, dtype=jnp.int32) == side
    cross_here = jnp.any(crosses & mine[None, :], axis=1)
    rank_here = jnp.sum(jnp.where(mine[None, :], rank, 0), axis=1)
    sent = jnp.sum(
        jnp.where((rank_here[None, :] == ids[:, None]) & cross_here[None, :], ids[None, :], 0),
        axis=1,
    )
    hit = dest_half[None, :, :] == (2 * ids + side)[:, None, None]
    from_other = jnp.any(hit & crosses[None], axis=(1, 2))
    place = jnp.sum(
        jnp.where(hit, jnp.where(crosses, rank, ids[:, None])[None], 0), axis=(1, 2)
    )
    return sent, from_other, place


def after(value, *earlier):
    return lax.optimization_barrier((value, earlier))[0]


def local(projections, grad_out, bias_q, half_kind, dest_half):
    dp_count = lax.axis_size("dp")
    seq_count = lax.axis_size("seq")
    dp_at = lax.axis_index("dp")
    seq_at = lax.axis_index("seq")
    rows, width = projections.shape
    q_width = bias_q.shape[0]
    kv_width = (width - q_width) // 2
    kv_heads = kv_width // HEAD
    span = seq_count // 2
    piece = seq_at % span
    bias = bias_q.reshape(1, q_width)
    factor = 1.0 / math.sqrt(rows * dp_count * seq_count)
    devices = dp_count * seq_count
    parts = 2
    heads = kv_heads // parts
    chips = dp_count // 2
    few = rows // dp_count
    chip, core = dp_at // 2, dp_at % 2
    chip_ids = jnp.arange(chips, dtype=jnp.int32)
    core_ids = jnp.arange(2, dtype=jnp.int32)
    swap = [(i, (i + span) % seq_count) for i in range(seq_count)]

    def later(by):
        return [(i, i + by) for i in range(seq_count) if i // span == (i + by) // span]

    def to_core(value):
        return lax.ppermute(value, "dp", [(i, i ^ 1) for i in range(dp_count)])

    def to_chip(value, by):
        return lax.ppermute(value, "dp", [(i, i ^ (2 * by)) for i in range(dp_count)])

    always = dp_count // 2
    sent_windows, from_other, place = plan(dest_half, seq_count)
    crossing = jnp.sum(dest_half[:, 0] % 2)
    step = max(1, always // 4)
    levels = list(range(0, always + 1, step))
    level = jnp.maximum(crossing - always + step - 1, 0) // step

    def window_source(window):
        by = (window // 2) ^ chip
        near = jnp.where(window % 2 == core, 0, 1)
        return jnp.where(by == 0, near, 1 + by), jnp.where(by == 0, chip, window % 2)

    leave = jnp.arange(1, chips, dtype=jnp.int32)[:, None] ^ chip
    leave_at = jnp.broadcast_to(leave, (chips - 1, 2)).reshape(-1)
    leave_from = jnp.broadcast_to(jnp.where(core_ids == core, 0, 1), (chips - 1, 2)).reshape(-1)
    leave_table = jnp.stack([leave_from, leave_at]).astype(jnp.int32)
    send_table = jnp.stack(window_source(sent_windows)).astype(jnp.int32)
    kept_from, kept_at = window_source(place)
    dest_from = jnp.where(from_other, 1 + chips + place // always, kept_from)
    dest_at = jnp.where(from_other, place % always, kept_at)
    by_chip = chip_ids[:, None] ^ chip == chip_ids[None, :]
    place_table = jnp.stack([
        jnp.sum(jnp.where(by_chip[:, :, None], t.reshape(1, chips, 2), 0), axis=1).reshape(-1)
        for t in (dest_from, dest_at)
    ]).astype(jnp.int32)
    back_table = jnp.stack([chip_ids ^ chip, jnp.full((chips,), 1, jnp.int32) - core])
    whole_table = jnp.stack([
        jnp.where(core_ids[:, None] == core, (chip_ids ^ chip)[None, :], chips).reshape(-1),
        jnp.where(core_ids[:, None] == core, core, chip_ids[None, :]).reshape(-1),
    ]).astype(jnp.int32)

    def spread(block):
        block, other = (x.reshape(chips, few, -1) for x in block)
        other = to_core(other)
        leaving = moved(leave_table, (2,) * (chips - 1), [block, other])
        return [block, other] + [to_chip(x, m + 1) for m, x in enumerate(leaving)], leaving

    def to_other_side(value):
        return lax.ppermute(value, "seq", swap)

    def first_sent(sources):
        return moved(send_table[:, :always], (always,), sources)[0]

    def rest(count, chunks):
        sent = [
            moved(send_table[:, always:], (count,), sources)[0] for sources in chunks if count
        ]
        return padded(
            always, [sources[0].shape[1:] for sources in chunks], [to_other_side(x) for x in sent]
        )

    def place_rows(sources):
        first, *leaving = moved(place_table, (2,) * chips, sources, far=1)
        held = [first] + [to_chip(x, m + 1) for m, x in enumerate(leaving)]
        (sent,) = moved(back_table, (chips,), held)
        return held + [to_core(sent)]

    kind = lax.dynamic_slice(half_kind, (dp_at, seq_at // span), (1, 1))[0, 0]
    seen = jnp.where(kind == 0, piece, piece % (span // 2))
    at = jnp.stack([seen, core]).astype(jnp.int32)
    earlier, before, own_kv = [], (), ()
    for part in range(parts):
        cols = slice(part * heads * HEAD, (part + 1) * heads * HEAD)
        rows_now = after(projections, *before)
        own_kv = jnp.stack(
            [rows_now[:, q_width + a : q_width + a + kv_width][:, cols] for a in (0, kv_width)]
        )
        pieces = [lax.ppermute(own_kv, "seq", later(d))[None] for d in range(1, span)]
        before = tuple(pieces)
        earlier.append(pieces[0] if span == 2 else jnp.concatenate(pieces))
    def with_later(own, off):
        for d in range(1, span):
            back = [(b, a) for a, b in later(d)]
            own = own + lax.ppermute(off[d - 1], "seq", back).astype(F32)
        return own.astype(BF16)

    def part_grads(part, at):
        *grad_query, own, q_sum, v_sum, off = attention(
            at, projections, grad_out, bias, earlier[part], part * heads, heads, q_width,
            vmem=12 if part else 56,
        )
        return grad_query, (own, off), (q_sum, v_sum)

    grad_query, pair, sums = part_grads(0, after(at, own_kv))
    grad_kv, all_sums = [with_later(*pair)], [sums]
    sources, leaving = spread(grad_query)
    chunks, crossed = [sources], []
    for part in range(1, parts):
        grad_query, pair, sums = part_grads(part, after(at, *leaving))
        all_sums.append(sums)
        sent = first_sent(chunks[-1])
        crossed.append(to_other_side(after(sent, *crossed[-1:])))
        sources, leaving = spread(after(grad_query, sent))
        chunks.append(sources)
        own, off = pair
        grad_kv.append(with_later(after(own, *leaving), off))
    last = jnp.concatenate([own[a] for a in (0, 1) for own in grad_kv], axis=1)
    first, second = last[: rows // 2], last[rows // 2 :]
    sources, leaving = spread(
        [jnp.where(core == 0, first, second), jnp.where(core == 0, second, first)]
    )
    sent = first_sent(after(chunks[-1], *leaving))
    crossed.append(to_other_side(after(sent, crossed[-1])))
    chunks.append(sources)
    sent = first_sent(after(sources, sent))
    crossed.append(to_other_side(after(sent, crossed[-1])))
    terms = jnp.concatenate(
        [
            jnp.concatenate([sums[i] for sums in all_sums], axis=1).reshape(devices, -1)
            for i in (0, 1)
        ],
        axis=1,
    )
    terms = lax.all_to_all(
        after(terms, sent), ("dp", "seq"), split_axis=0, concat_axis=0, tiled=True
    )
    terms = jnp.sum(terms, axis=0) * factor
    more = lax.switch(after(level, sent), [partial(rest, n) for n in levels], chunks)
    crossed[1] = after(crossed[1], terms)
    placed = [
        place_rows([*sources, now, then]) for sources, now, then in zip(chunks, crossed, more)
    ]
    whole = joined(whole_table, placed)
    return (
        whole.reshape(rows, width),
        terms[: q_width // devices],
        terms[q_width // devices :],
    )


def solution(mesh):
    in_specs = (P(("dp", "seq"), None), P(("dp", "seq"), None), P(), P(), P())
    out_specs = (P(("dp", "seq"), None), P(("dp", "seq")), P(("dp", "seq")))
    return jax.shard_map(local, mesh=mesh, in_specs=in_specs, out_specs=out_specs, check_vma=False)
```

```python
import math
from functools import partial, reduce

import jax
import jax.numpy as jnp
from jax import lax
from jax.experimental import pallas as pl
from jax.experimental.pallas import tpu as pltpu
from jax.sharding import PartitionSpec as P

HEAD = 128
NEG = -1e30
SWAP_FLOPS = 10**10
PLACE_FLOPS = 17 * 10**8
F32 = jnp.float32
BF16 = jnp.bfloat16
SCALE = 1.0 / math.sqrt(HEAD)


def dot(a, b, a_dim, b_dim):
    return lax.dot_general(a, b, (((a_dim,), (b_dim,)), ((), ())), preferred_element_type=F32)


def attention_kernel(
    group_size, earlier, at_ref, q_ref, k_ref, v_ref, grad_ref, bias_ref, *refs
):
    kv_off_ref = refs[0] if earlier else None
    outs = refs[1:] if earlier else refs
    dq_ref, dkv_ref, q_sum_ref, v_sum_ref = outs[:4]
    off_ref = outs[4] if earlier else None
    rows = q_ref.shape[0]

    keys = [k_ref[...]] + [kv_off_ref[d, 0] for d in range(earlier)]
    values = [v_ref[...]] + [kv_off_ref[d, 1] for d in range(earlier)]
    key_at = lax.broadcasted_iota(jnp.int32, (rows, rows), 0)
    query_at = lax.broadcasted_iota(jnp.int32, (rows, rows), 1)
    allowed = [key_at <= query_at] + [at_ref[0] > d for d in range(earlier)]

    def one_head(head, sums):
        grad_keys, grad_values = sums
        cols = slice(head * HEAD, (head + 1) * HEAD)
        query = (q_ref[:, cols].astype(F32) + bias_ref[:, cols].astype(F32)).astype(BF16)
        grad = grad_ref[:, cols]
        scores = [jnp.where(ok, dot(key, query, 1, 1), NEG) for ok, key in zip(allowed, keys)]
        tops = [jnp.max(s, axis=0, keepdims=True) for s in scores]
        top = reduce(jnp.maximum, tops)
        exps = [jnp.exp((s - top) * SCALE) for s in scores]
        grad_probs = [dot(value, grad, 1, 1) for value in values]
        total = sum(jnp.sum(e, axis=0, keepdims=True) for e in exps)
        mixed = sum(jnp.sum(e * g, axis=0, keepdims=True) for e, g in zip(exps, grad_probs))
        inverse = 1.0 / total
        delta = mixed * inverse
        scaled = inverse * SCALE
        weights = [(e * inverse).astype(BF16) for e in exps]
        grad_scores = [(e * scaled * (g - delta)).astype(BF16) for e, g in zip(exps, grad_probs)]
        grad_values = [t + dot(w, grad, 1, 0) for t, w in zip(grad_values, weights)]
        grad_keys = [t + dot(s, query, 1, 0) for t, s in zip(grad_keys, grad_scores)]
        grad_query = sum(dot(s, key, 0, 0) for s, key in zip(grad_scores, keys))
        dq_ref[:, cols] = grad_query.astype(BF16)
        q_sum_ref[:, cols] = jnp.sum(grad_query, axis=0, keepdims=True)
        return grad_keys, grad_values

    zeros = [jnp.zeros((rows, HEAD), F32) for _ in keys]
    sums = (zeros, zeros)
    for head in range(group_size):
        sums = one_head(head, sums)
    grad_keys, grad_values = sums
    dkv_ref[0] = grad_keys[0]
    dkv_ref[1] = grad_values[0]
    v_sum_ref[...] = sum(jnp.sum(g, axis=0, keepdims=True) for g in grad_values)
    for d in range(earlier):
        off_ref[d, 0] = grad_keys[d + 1].astype(BF16)
        off_ref[d, 1] = grad_values[d + 1].astype(BF16)


def attention(at, projections, grad_out, bias, kv_off, skip, first, groups, q_width, vmem):
    rows, width = projections.shape
    kv_width = (width - q_width) // 2
    group_size = q_width // kv_width
    earlier = kv_off.shape[0]
    wide = group_size * HEAD
    k_at = q_width // HEAD + first
    v_at = k_at + kv_width // HEAD
    in_specs = [
        pl.BlockSpec((rows, wide), lambda g, s: (0, first + g)),
        pl.BlockSpec((rows, HEAD), lambda g, s: (0, k_at + g)),
        pl.BlockSpec((rows, HEAD), lambda g, s: (0, v_at + g)),
        pl.BlockSpec((rows, wide), lambda g, s: (0, first + g)),
        pl.BlockSpec((1, wide), lambda g, s: (0, first + g)),
    ]
    operands = [projections, projections, projections, grad_out, bias]
    if earlier:
        in_specs.append(
            pl.BlockSpec((earlier, 2, rows, HEAD), lambda g, s: (0, 0, 0, skip + g))
        )
        operands.append(kv_off)
    out_specs = [
        pl.BlockSpec((rows, wide), lambda g, s: (0, g)),
        pl.BlockSpec((2, rows, HEAD), lambda g, s: (0, 0, g)),
        pl.BlockSpec((1, wide), lambda g, s: (0, g)),
        pl.BlockSpec((1, HEAD), lambda g, s: (0, g)),
    ]
    out_shape = [
        jax.ShapeDtypeStruct((rows, groups * wide), BF16),
        jax.ShapeDtypeStruct((2, rows, groups * HEAD), F32),
        jax.ShapeDtypeStruct((1, groups * wide), F32),
        jax.ShapeDtypeStruct((1, groups * HEAD), F32),
    ]
    if earlier:
        out_specs.append(pl.BlockSpec((earlier, 2, rows, HEAD), lambda g, s: (0, 0, 0, g)))
        out_shape.append(jax.ShapeDtypeStruct((earlier, 2, rows, groups * HEAD), BF16))
    flops = 10 * groups * group_size * rows * rows * HEAD * (1 + earlier)
    outs = pl.pallas_call(
        partial(attention_kernel, group_size, earlier),
        grid_spec=pltpu.PrefetchScalarGridSpec(
            num_scalar_prefetch=1, grid=(groups,), in_specs=in_specs, out_specs=out_specs
        ),
        out_shape=out_shape,
        compiler_params=pltpu.CompilerParams(vmem_limit_bytes=vmem * 1024 * 1024),
        cost_estimate=pl.CostEstimate(
            flops=flops,
            bytes_accessed=4 * rows * groups * wide,
            transcendentals=groups * group_size * rows * rows * (1 + earlier),
        ),
        name="attention_grads",
    )(at, *operands)
    return outs if earlier else (*outs, None)


def move_kernel(shape, groups, far, start, places_ref, *refs):
    *refs, sem = refs
    sources, outs = refs[: len(refs) - len(shape)], refs[len(refs) - len(shape) :]
    each = len(sources) // groups
    first = 0
    for out_ref, count in zip(outs, shape):

        def fill(j, _, out_ref=out_ref, first=first):
            for at in range(each):

                @pl.when(places_ref[0, first + j] == at)
                def _():
                    column = 0
                    for source in sources[at::each]:
                        wide = min(source.shape[-1] - start, out_ref.shape[-1])
                        cols, taken = pl.ds(column, wide), pl.ds(start, wide)
                        index = places_ref[1, first + j]
                        if at < each - far:
                            out_ref[j, :, cols] = source[index, :, taken]
                        else:
                            copy = pltpu.make_async_copy(
                                source.at[index, :, taken], out_ref.at[j, :, cols], sem
                            )
                            copy.start()
                            copy.wait()
                        column += wide

            return 0

        lax.fori_loop(0, count, fill, 0)
        first += count


def moved(places, shape, *groups, far=0, flops=1, start=0, width=None):
    vmem = pl.BlockSpec(memory_space=pltpu.VMEM)
    where = [vmem] * (len(groups[0]) - far) + [pl.BlockSpec(memory_space=pl.ANY)] * far
    rows = groups[0][0].shape[1]
    width = width or sum(sources[0].shape[2] for sources in groups)
    return pl.pallas_call(
        partial(move_kernel, shape, len(groups), far, start),
        in_specs=[pl.BlockSpec(memory_space=pltpu.SMEM)] + where * len(groups),
        out_specs=[vmem for _ in shape],
        out_shape=[jax.ShapeDtypeStruct((n, rows, width), BF16) for n in shape],
        scratch_shapes=[pltpu.SemaphoreType.DMA],
        compiler_params=pltpu.CompilerParams(vmem_limit_bytes=10 * 1024 * 1024),
        cost_estimate=pl.CostEstimate(flops=flops, bytes_accessed=1, transcendentals=0),
        name="move_slices",
    )(places, *[source for sources in groups for source in sources])


def pad_kernel(*refs):
    for got_ref, out_ref in zip(refs[: len(refs) // 2], refs[len(refs) // 2 :]):
        out_ref[: got_ref.shape[0]] = got_ref[...]


def padded(size, shapes, gots):
    vmem = pl.BlockSpec(memory_space=pltpu.VMEM)
    return pl.pallas_call(
        pad_kernel if gots else lambda *outs: None,
        in_specs=[vmem for _ in gots],
        out_specs=[vmem if gots else pl.BlockSpec(memory_space=pl.ANY) for _ in shapes],
        out_shape=[jax.ShapeDtypeStruct((size, *shape), BF16) for shape in shapes],
        compiler_params=pltpu.CompilerParams(vmem_limit_bytes=10 * 1024 * 1024),
        name="pad_slices",
    )(*gots)


def join_kernel(parts, places_ref, *refs):
    sources, out_ref, sem = refs[:-2], refs[-2], refs[-1]
    each = len(sources) // len(parts)
    count = out_ref.shape[0]
    for wait in (False, True):
        column = 0
        for chunk, (wide, start) in enumerate(parts):
            for i in range(count):
                to = out_ref.at[i, :, pl.ds(column, wide)]
                done = sem.at[chunk * count + i]
                if wait:
                    pltpu.make_async_copy(to, to, done).wait()
                    continue
                for at, source in enumerate(sources[chunk * each : (chunk + 1) * each]):
                    taken = pl.ds(start if at < each - 1 else 0, wide)

                    @pl.when(places_ref[0, i] == at)
                    def _():
                        pltpu.make_async_copy(
                            source.at[places_ref[1, i], :, taken], to, done
                        ).start()

            column += wide


def joined(places, chunks):
    count, rows = places.shape[1], chunks[0][0][0].shape[1]
    parts = [(sources[-1].shape[-1], start) for sources, start in chunks]
    vmem = pl.BlockSpec(memory_space=pltpu.VMEM)
    operands = [x for sources, _ in chunks for x in sources]
    return pl.pallas_call(
        partial(join_kernel, parts),
        in_specs=[pl.BlockSpec(memory_space=pltpu.SMEM)] + [vmem for _ in operands],
        out_specs=pl.BlockSpec(memory_space=pl.ANY),
        out_shape=jax.ShapeDtypeStruct((count, rows, sum(wide for wide, _ in parts)), BF16),
        scratch_shapes=[pltpu.SemaphoreType.DMA((count * len(parts),))],
        compiler_params=pltpu.CompilerParams(vmem_limit_bytes=10 * 1024 * 1024),
        cost_estimate=pl.CostEstimate(flops=1, bytes_accessed=1, transcendentals=0),
        name="join_chunks",
    )(places, *operands)


def plan(dest_half, seq_count):
    windows = dest_half.shape[0]
    ids = jnp.arange(windows, dtype=jnp.int32)
    side = lax.axis_index("seq") // (seq_count // 2)
    crosses = (dest_half % 2) != jnp.arange(2, dtype=jnp.int32)[None, :]
    rank = jnp.sum(
        jnp.where((ids[None, :] < ids[:, None])[:, :, None], crosses[None, :, :], False), axis=1
    ).astype(jnp.int32)
    mine = jnp.arange(2, dtype=jnp.int32) == side
    cross_here = jnp.any(crosses & mine[None, :], axis=1)
    rank_here = jnp.sum(jnp.where(mine[None, :], rank, 0), axis=1)
    sent = jnp.sum(
        jnp.where((rank_here[None, :] == ids[:, None]) & cross_here[None, :], ids[None, :], 0),
        axis=1,
    )
    hit = dest_half[None, :, :] == (2 * ids + side)[:, None, None]
    from_other = jnp.any(hit & crosses[None], axis=(1, 2))
    place = jnp.sum(
        jnp.where(hit, jnp.where(crosses, rank, ids[:, None])[None], 0), axis=(1, 2)
    )
    return sent, from_other, place


def after(value, *earlier):
    return lax.optimization_barrier((value, earlier))[0]


def local(projections, grad_out, bias_q, half_kind, dest_half):
    dp_count = lax.axis_size("dp")
    seq_count = lax.axis_size("seq")
    dp_at = lax.axis_index("dp")
    seq_at = lax.axis_index("seq")
    rows, width = projections.shape
    q_width = bias_q.shape[0]
    kv_width = (width - q_width) // 2
    kv_heads = kv_width // HEAD
    span = seq_count // 2
    piece = seq_at % span
    bias = bias_q.reshape(1, q_width)
    factor = 1.0 / math.sqrt(rows * dp_count * seq_count)
    devices = dp_count * seq_count
    parts = [kv_heads // 2, kv_heads - kv_heads // 2]
    chips = dp_count // 2
    few = rows // dp_count
    chip, core = dp_at // 2, dp_at % 2
    chip_ids = jnp.arange(chips, dtype=jnp.int32)
    core_ids = jnp.arange(2, dtype=jnp.int32)
    swap = [(i, (i + span) % seq_count) for i in range(seq_count)]

    def later(by):
        return [(i, i + by) for i in range(seq_count) if i // span == (i + by) // span]

    def to_core(value):
        return lax.ppermute(value, "dp", [(i, i ^ 1) for i in range(dp_count)])

    def to_chip(value, by):
        return lax.ppermute(value, "dp", [(i, i ^ (2 * by)) for i in range(dp_count)])

    always = dp_count // 2
    sent_windows, from_other, place = plan(dest_half, seq_count)
    crossing = jnp.sum(dest_half[:, 0] % 2)
    step = max(1, always // 4)
    levels = list(range(0, always + 1, step))
    level = jnp.maximum(crossing - always + step - 1, 0) // step

    send_table = jnp.stack([jnp.zeros_like(sent_windows), sent_windows])
    dest_from = jnp.where(from_other, 1 + place // always, 0)
    dest_at = jnp.where(from_other, place % always, place)
    by_chip = chip_ids[:, None] ^ chip == chip_ids[None, :]
    place_table = jnp.stack([
        jnp.sum(jnp.where(by_chip[:, :, None], t.reshape(1, chips, 2), 0), axis=1).reshape(-1)
        for t in (dest_from, dest_at)
    ]).astype(jnp.int32)
    back_table = jnp.stack([chip_ids ^ chip, jnp.full((chips,), 1, jnp.int32) - core])
    near = core_ids[None, :] == core
    whole_table = jnp.stack([
        jnp.where(near, (chip_ids ^ chip)[:, None], chips).reshape(-1),
        jnp.where(near, core, chip_ids[:, None]).reshape(-1),
    ]).astype(jnp.int32)

    def spread(block):
        slices = block.reshape(dp_count, few, -1)
        return lax.all_to_all(slices, "dp", split_axis=0, concat_axis=0, tiled=True)

    def by_distance(values, at):
        ids = jnp.arange(values.shape[0], dtype=jnp.int32)
        hit = (ids[:, None] ^ ids[None, :]) == at
        hit = hit.reshape(hit.shape + (1,) * (values.ndim - 1))
        return jnp.sum(jnp.where(hit, values[None], 0), axis=1)

    def summed_dp(shares):
        shares = shares.reshape(chips, 2, seq_count, -1)
        shares = by_distance(shares.swapaxes(0, 1), core)
        shares = shares[0] + to_core(shares[1])
        shares = by_distance(shares, chip)
        return sum([to_chip(shares[m], m) for m in range(1, chips)], shares[0])

    def summed_seq(shares):
        shares = by_distance(shares, seq_at)
        pairs = [[(i, i ^ m) for i in range(seq_count)] for m in range(seq_count)]
        return sum(
            [lax.ppermute(shares[m], "seq", pairs[m]) for m in range(1, seq_count)], shares[0]
        )

    def to_other_side(value):
        return lax.ppermute(value, "seq", swap)

    def first_sent(sources):
        return moved(send_table[:, :always], (always,), [sources], flops=SWAP_FLOPS)[0]

    def rest(count, chunks):
        sent = [
            moved(send_table[:, always:], (count,), [chunk])[0] for chunk in chunks if count
        ]
        return padded(
            always, [chunk.shape[1:] for chunk in chunks], [to_other_side(x) for x in sent]
        )

    def place_rows(*groups, flops=1):
        first, *leaving = moved(place_table, (2,) * chips, *groups, far=1, flops=flops)
        return [first] + [to_chip(x, m + 1) for m, x in enumerate(leaving)]

    kind = lax.dynamic_slice(half_kind, (dp_at, seq_at // span), (1, 1))[0, 0]
    seen = jnp.where(kind == 0, piece, piece % (span // 2))
    at = seen.reshape(1).astype(jnp.int32)
    def earlier_kv(source, first, count):
        cols = slice(first * HEAD, (first + count) * HEAD)
        own = [source[:, q_width + a : q_width + a + kv_width][:, cols] for a in (0, kv_width)]
        own = jnp.stack(own)
        pieces = [lax.ppermute(own, "seq", later(d))[None] for d in range(1, span)]
        return pieces[0] if span == 2 else jnp.concatenate(pieces), own

    kv_first, own_first = earlier_kv(projections, 0, parts[0])
    kv_rest, _ = earlier_kv(after(projections, own_first), parts[0], kv_heads - parts[0])

    def back_to_owners(off):
        return [
            lax.ppermute(off[d - 1], "seq", [(b, a) for a, b in later(d)]) for d in range(1, span)
        ]

    def part_grads(part, at):
        first = sum(parts[:part])
        grad_query, own, q_sum, v_sum, off = attention(
            at,
            projections,
            grad_out,
            bias,
            kv_rest if part else kv_first,
            first - parts[0] if part else 0,
            first,
            parts[part],
            q_width,
            vmem=12 if part else 56,
        )
        return grad_query, own, off, (q_sum, v_sum)

    grad_query, own, off, sums = part_grads(0, after(at, send_table, place_table, whole_table))
    owns, parcels, all_sums = [own], [back_to_owners(off)], [sums]
    chunks, crossed = [spread(after(grad_query, kv_rest))], []
    for part in range(1, len(parts)):
        grad_query, own, off, sums = part_grads(part, after(at, grad_query))
        sent = first_sent(after(chunks[-1], own, parcels[-1], *crossed[-1:]))
        owns.append(own)
        parcels.append(back_to_owners(off))
        all_sums.append(sums)
        crossed.append(to_other_side(sent))
        chunks.append(spread(after(grad_query, sent)))
    terms = jnp.concatenate(
        [
            jnp.concatenate([sums[i] for sums in all_sums], axis=1).reshape(devices, -1)
            for i in (0, 1)
        ],
        axis=1,
    )
    terms = summed_dp(after(terms, sent))
    parcel = [jnp.concatenate(x, axis=-1).astype(F32) for x in zip(*parcels)]
    own = jnp.concatenate(after(owns, chunks[-1]), axis=-1)
    own = sum(parcel, own).astype(BF16)
    last = jnp.concatenate([own[0], own[1]], axis=1)
    sent = first_sent(after(chunks[-1], crossed[-1], last, terms))
    crossed.append(to_other_side(sent))
    chunks.append(spread(after(last, sent)))
    terms = summed_seq(after(terms, sent)) * factor
    sent = first_sent(after(chunks[-1], crossed[-1], terms))
    crossed.append(to_other_side(sent))
    more = lax.switch(after(level, sent), [partial(rest, n) for n in levels], chunks)
    groups = [list(group) for group in zip(chunks, crossed, more)]
    held = place_rows(*after(groups[:-1], sent))
    held_last = place_rows(groups[-1], flops=PLACE_FLOPS)
    held = after(held, held_last[0])
    pieces, start = [], 0
    for group in groups[:-1]:
        wide = group[0].shape[-1]
        (returned,) = moved(back_table, (chips,), held, start=start, width=wide)
        pieces.append((held + [to_core(returned)], start))
        start += wide
    (returned,) = moved(back_table, (chips,), held_last)
    pieces.append((held_last + [to_core(returned)], 0))
    whole = joined(whole_table, pieces)
    return (
        whole.reshape(rows, width),
        terms[: q_width // devices],
        terms[q_width // devices :],
    )


def solution(mesh):
    in_specs = (P(("dp", "seq"), None), P(("dp", "seq"), None), P(), P(), P())
    out_specs = (P(("dp", "seq"), None), P(("dp", "seq")), P(("dp", "seq")))
    return jax.shard_map(local, mesh=mesh, in_specs=in_specs, out_specs=out_specs, check_vma=False)
```

```python
import math
from functools import partial, reduce

import jax
import jax.numpy as jnp
from jax import lax
from jax.experimental import pallas as pl
from jax.experimental.pallas import tpu as pltpu
from jax.sharding import PartitionSpec as P

HEAD = 128
NEG = -1e30
SWAP_FLOPS = 10**10
GATE_FLOPS = 6 * 10**9
PLACE_FLOPS = 17 * 10**8
F32 = jnp.float32
BF16 = jnp.bfloat16
SCALE = 1.0 / math.sqrt(HEAD)
LOG2_E = math.log2(math.e)


def dot(a, b, a_dim, b_dim):
    return lax.dot_general(a, b, (((a_dim,), (b_dim,)), ((), ())), preferred_element_type=F32)


def attention_kernel(
    group_size, earlier, at_ref, q_ref, k_ref, v_ref, grad_ref, bias_ref, *refs
):
    kv_off_ref = refs[0] if earlier else None
    outs = refs[1:] if earlier else refs
    dq_ref, dkv_ref, q_sum_ref, v_sum_ref = outs[:4]
    off_ref = outs[4] if earlier else None
    rows = q_ref.shape[0]

    keys = [k_ref[...]] + [kv_off_ref[d, 0] for d in range(earlier)]
    values = [v_ref[...]] + [kv_off_ref[d, 1] for d in range(earlier)]
    key_at = lax.broadcasted_iota(jnp.int32, (rows, rows), 0)
    query_at = lax.broadcasted_iota(jnp.int32, (rows, rows), 1)
    allowed = [key_at <= query_at] + [at_ref[0] > d for d in range(earlier)]

    def one_head(head, sums):
        grad_keys, grad_values = sums
        cols = slice(head * HEAD, (head + 1) * HEAD)
        query = (q_ref[:, cols].astype(F32) + bias_ref[:, cols].astype(F32)).astype(BF16)
        grad = grad_ref[:, cols]
        scores = [jnp.where(ok, dot(key, query, 1, 1), NEG) for ok, key in zip(allowed, keys)]
        tops = [jnp.max(s, axis=0, keepdims=True) for s in scores]
        top = reduce(jnp.maximum, tops)
        exps = [jnp.exp2((s - top) * (SCALE * LOG2_E)) for s in scores]
        grad_probs = [dot(value, grad, 1, 1) for value in values]
        total = sum(jnp.sum(e, axis=0, keepdims=True) for e in exps)
        mixed = sum(jnp.sum(e * g, axis=0, keepdims=True) for e, g in zip(exps, grad_probs))
        inverse = 1.0 / total
        delta = mixed * inverse
        scaled = inverse * SCALE
        weights = [(e * inverse).astype(BF16) for e in exps]
        grad_scores = [(e * scaled * (g - delta)).astype(BF16) for e, g in zip(exps, grad_probs)]
        grad_values = [t + dot(w, grad, 1, 0) for t, w in zip(grad_values, weights)]
        grad_keys = [t + dot(s, query, 1, 0) for t, s in zip(grad_keys, grad_scores)]
        grad_query = sum(dot(s, key, 0, 0) for s, key in zip(grad_scores, keys))
        dq_ref[:, cols] = grad_query.astype(BF16)
        q_sum_ref[:, cols] = jnp.sum(grad_query, axis=0, keepdims=True)
        return grad_keys, grad_values

    zeros = [jnp.zeros((rows, HEAD), F32) for _ in keys]
    sums = (zeros, zeros)
    for head in range(group_size):
        sums = one_head(head, sums)
    grad_keys, grad_values = sums
    dkv_ref[0] = grad_keys[0]
    dkv_ref[1] = grad_values[0]
    v_sum_ref[...] = sum(jnp.sum(g, axis=0, keepdims=True) for g in grad_values)
    for d in range(earlier):
        off_ref[d, 0] = grad_keys[d + 1].astype(BF16)
        off_ref[d, 1] = grad_values[d + 1].astype(BF16)


def attention(at, projections, grad_out, bias, kv_off, skip, first, groups, q_width, vmem):
    rows, width = projections.shape
    kv_width = (width - q_width) // 2
    group_size = q_width // kv_width
    earlier = kv_off.shape[0]
    wide = group_size * HEAD
    k_at = q_width // HEAD + first
    v_at = k_at + kv_width // HEAD
    in_specs = [
        pl.BlockSpec((rows, wide), lambda g, s: (0, first + g)),
        pl.BlockSpec((rows, HEAD), lambda g, s: (0, k_at + g)),
        pl.BlockSpec((rows, HEAD), lambda g, s: (0, v_at + g)),
        pl.BlockSpec((rows, wide), lambda g, s: (0, first + g)),
        pl.BlockSpec((1, wide), lambda g, s: (0, first + g)),
    ]
    operands = [projections, projections, projections, grad_out, bias]
    if earlier:
        in_specs.append(
            pl.BlockSpec((earlier, 2, rows, HEAD), lambda g, s: (0, 0, 0, skip + g))
        )
        operands.append(kv_off)
    out_specs = [
        pl.BlockSpec((rows, wide), lambda g, s: (0, g)),
        pl.BlockSpec((2, rows, HEAD), lambda g, s: (0, 0, g)),
        pl.BlockSpec((1, wide), lambda g, s: (0, g)),
        pl.BlockSpec((1, HEAD), lambda g, s: (0, g)),
    ]
    out_shape = [
        jax.ShapeDtypeStruct((rows, groups * wide), BF16),
        jax.ShapeDtypeStruct((2, rows, groups * HEAD), F32),
        jax.ShapeDtypeStruct((1, groups * wide), F32),
        jax.ShapeDtypeStruct((1, groups * HEAD), F32),
    ]
    if earlier:
        out_specs.append(pl.BlockSpec((earlier, 2, rows, HEAD), lambda g, s: (0, 0, 0, g)))
        out_shape.append(jax.ShapeDtypeStruct((earlier, 2, rows, groups * HEAD), BF16))
    flops = 10 * groups * group_size * rows * rows * HEAD * (1 + earlier)
    outs = pl.pallas_call(
        partial(attention_kernel, group_size, earlier),
        grid_spec=pltpu.PrefetchScalarGridSpec(
            num_scalar_prefetch=1, grid=(groups,), in_specs=in_specs, out_specs=out_specs
        ),
        out_shape=out_shape,
        compiler_params=pltpu.CompilerParams(vmem_limit_bytes=vmem * 1024 * 1024),
        cost_estimate=pl.CostEstimate(
            flops=flops,
            bytes_accessed=4 * rows * groups * wide,
            transcendentals=groups * group_size * rows * rows * (1 + earlier),
        ),
        name="attention_grads",
    )(at, *operands)
    return outs if earlier else (*outs, None)


def move_kernel(shape, widths, far, start, places_ref, *refs):
    *refs, sem = refs
    sources, outs = refs[: len(refs) - len(shape)], refs[len(refs) - len(shape) :]
    each = len(sources) // len(widths)
    first = 0
    for out_ref, count in zip(outs, shape):

        def fill(j, _, out_ref=out_ref, first=first):
            for at in range(each):

                @pl.when(places_ref[0, first + j] == at)
                def _():
                    column = 0
                    for source, wide in zip(sources[at::each], widths):
                        cols, taken = pl.ds(column, wide), pl.ds(start, wide)
                        index = places_ref[1, first + j]
                        if at < each - far:
                            out_ref[j, :, cols] = source[index, :, taken]
                        else:
                            copy = pltpu.make_async_copy(
                                source.at[index, :, taken], out_ref.at[j, :, cols], sem
                            )
                            copy.start()
                            copy.wait()
                        column += wide

            return 0

        lax.fori_loop(0, count, fill, 0)
        first += count


def moved(places, shape, *groups, far=0, flops=1, start=0, widths=None):
    vmem = pl.BlockSpec(memory_space=pltpu.VMEM)
    where = [vmem] * (len(groups[0]) - far) + [pl.BlockSpec(memory_space=pl.ANY)] * far
    rows = groups[0][0].shape[1]
    widths = widths or [sources[-1].shape[2] for sources in groups]
    width = sum(widths)
    return pl.pallas_call(
        partial(move_kernel, shape, widths, far, start),
        in_specs=[pl.BlockSpec(memory_space=pltpu.SMEM)] + where * len(groups),
        out_specs=[vmem for _ in shape],
        out_shape=[jax.ShapeDtypeStruct((n, rows, width), BF16) for n in shape],
        scratch_shapes=[pltpu.SemaphoreType.DMA],
        compiler_params=pltpu.CompilerParams(vmem_limit_bytes=10 * 1024 * 1024),
        cost_estimate=pl.CostEstimate(flops=flops, bytes_accessed=1, transcendentals=0),
        name="move_slices",
    )(places, *[source for sources in groups for source in sources])


def pad_kernel(*refs):
    for got_ref, out_ref in zip(refs[: len(refs) // 2], refs[len(refs) // 2 :]):
        out_ref[: got_ref.shape[0]] = got_ref[...]


def padded(size, shapes, gots):
    vmem = pl.BlockSpec(memory_space=pltpu.VMEM)
    return pl.pallas_call(
        pad_kernel if gots else lambda *outs: None,
        in_specs=[vmem for _ in gots],
        out_specs=[vmem if gots else pl.BlockSpec(memory_space=pl.ANY) for _ in shapes],
        out_shape=[jax.ShapeDtypeStruct((size, *shape), BF16) for shape in shapes],
        compiler_params=pltpu.CompilerParams(vmem_limit_bytes=10 * 1024 * 1024),
        name="pad_slices",
    )(*gots)


def join_kernel(parts, places_ref, *refs):
    sources, out_ref, sem = refs[:-2], refs[-2], refs[-1]
    each = len(sources) // len(parts)
    count = out_ref.shape[0]
    for wait in (False, True):
        column = 0
        for chunk, (wide, start) in enumerate(parts):
            for i in range(count):
                to = out_ref.at[i, :, pl.ds(column, wide)]
                done = sem.at[chunk * count + i]
                if wait:
                    pltpu.make_async_copy(to, to, done).wait()
                    continue
                for at, source in enumerate(sources[chunk * each : (chunk + 1) * each]):
                    taken = pl.ds(start if at < each - 1 else 0, wide)

                    @pl.when(places_ref[0, i] == at)
                    def _():
                        pltpu.make_async_copy(
                            source.at[places_ref[1, i], :, taken], to, done
                        ).start()

            column += wide


def joined(places, chunks):
    count, rows = places.shape[1], chunks[0][0][0].shape[1]
    parts = [(sources[-1].shape[-1], start) for sources, start in chunks]
    vmem = pl.BlockSpec(memory_space=pltpu.VMEM)
    operands = [x for sources, _ in chunks for x in sources]
    return pl.pallas_call(
        partial(join_kernel, parts),
        in_specs=[pl.BlockSpec(memory_space=pltpu.SMEM)] + [vmem for _ in operands],
        out_specs=pl.BlockSpec(memory_space=pl.ANY),
        out_shape=jax.ShapeDtypeStruct((count, rows, sum(wide for wide, _ in parts)), BF16),
        scratch_shapes=[pltpu.SemaphoreType.DMA((count * len(parts),))],
        compiler_params=pltpu.CompilerParams(vmem_limit_bytes=10 * 1024 * 1024),
        cost_estimate=pl.CostEstimate(flops=1, bytes_accessed=1, transcendentals=0),
        name="join_chunks",
    )(places, *operands)


def beside_kernel(block_ref, values_ref, out_ref):
    wide, count = block_ref.shape[-1], values_ref.shape[1]
    out_ref[:, :, :wide] = block_ref[...]
    out_ref[:, :, wide:] = jnp.zeros((*block_ref.shape[:2], HEAD), BF16)
    rest = values_ref[...]
    for part in range(3):
        piece = rest.astype(BF16)
        out_ref[:, part * count : (part + 1) * count, wide:] = piece
        rest = rest - piece.astype(F32)


def beside(block, values):
    vmem = pl.BlockSpec(memory_space=pltpu.VMEM)
    return pl.pallas_call(
        beside_kernel,
        in_specs=[vmem, vmem],
        out_specs=vmem,
        out_shape=jax.ShapeDtypeStruct((*block.shape[:2], block.shape[2] + HEAD), BF16),
        compiler_params=pltpu.CompilerParams(vmem_limit_bytes=10 * 1024 * 1024),
        cost_estimate=pl.CostEstimate(flops=GATE_FLOPS, bytes_accessed=1, transcendentals=0),
        name="beside",
    )(block, values)


def plan(dest_half, seq_count):
    windows = dest_half.shape[0]
    ids = jnp.arange(windows, dtype=jnp.int32)
    side = lax.axis_index("seq") // (seq_count // 2)
    crosses = (dest_half % 2) != jnp.arange(2, dtype=jnp.int32)[None, :]
    rank = jnp.sum(
        jnp.where((ids[None, :] < ids[:, None])[:, :, None], crosses[None, :, :], False), axis=1
    ).astype(jnp.int32)
    mine = jnp.arange(2, dtype=jnp.int32) == side
    cross_here = jnp.any(crosses & mine[None, :], axis=1)
    rank_here = jnp.sum(jnp.where(mine[None, :], rank, 0), axis=1)
    sent = jnp.sum(
        jnp.where((rank_here[None, :] == ids[:, None]) & cross_here[None, :], ids[None, :], 0),
        axis=1,
    )
    hit = dest_half[None, :, :] == (2 * ids + side)[:, None, None]
    from_other = jnp.any(hit & crosses[None], axis=(1, 2))
    place = jnp.sum(
        jnp.where(hit, jnp.where(crosses, rank, ids[:, None])[None], 0), axis=(1, 2)
    )
    return sent, from_other, place


def after(value, *earlier):
    return lax.optimization_barrier((value, earlier))[0]


def gate_kernel(in_ref, out_ref):
    out_ref[...] = in_ref[...]


def gate(value, *earlier):
    return pl.pallas_call(
        gate_kernel,
        out_shape=jax.ShapeDtypeStruct(value.shape, value.dtype),
        cost_estimate=pl.CostEstimate(flops=GATE_FLOPS, bytes_accessed=1, transcendentals=0),
        name="gate",
    )(after(value, *earlier))


def local(projections, grad_out, bias_q, half_kind, dest_half):
    dp_count = lax.axis_size("dp")
    seq_count = lax.axis_size("seq")
    dp_at = lax.axis_index("dp")
    seq_at = lax.axis_index("seq")
    rows, width = projections.shape
    q_width = bias_q.shape[0]
    kv_width = (width - q_width) // 2
    kv_heads = kv_width // HEAD
    span = seq_count // 2
    piece = seq_at % span
    bias = bias_q.reshape(1, q_width)
    factor = 1.0 / math.sqrt(rows * dp_count * seq_count)
    devices = dp_count * seq_count
    parts = [kv_heads // 2, kv_heads - kv_heads // 2]
    chips = dp_count // 2
    few = rows // dp_count
    chip, core = dp_at // 2, dp_at % 2
    chip_ids = jnp.arange(chips, dtype=jnp.int32)
    core_ids = jnp.arange(2, dtype=jnp.int32)
    swap = [(i, (i + span) % seq_count) for i in range(seq_count)]

    def later(by):
        return [(i, i + by) for i in range(seq_count) if i // span == (i + by) // span]

    def to_core(value):
        return lax.ppermute(value, "dp", [(i, i ^ 1) for i in range(dp_count)])

    def to_chip(value, by):
        return lax.ppermute(value, "dp", [(i, i ^ (2 * by)) for i in range(dp_count)])

    always = dp_count // 2
    sent_windows, from_other, place = plan(dest_half, seq_count)
    crossing = jnp.sum(dest_half[:, 0] % 2)
    step = max(1, always // 4)
    levels = list(range(0, always + 1, step))
    level = jnp.maximum(crossing - always + step - 1, 0) // step

    send_table = jnp.stack([jnp.zeros_like(sent_windows), sent_windows])
    dest_from = jnp.where(from_other, 1 + place // always, 0)
    dest_at = jnp.where(from_other, place % always, place)
    by_chip = chip_ids[:, None] ^ chip == chip_ids[None, :]
    place_table = jnp.stack([
        jnp.sum(jnp.where(by_chip[:, :, None], t.reshape(1, chips, 2), 0), axis=1).reshape(-1)
        for t in (dest_from, dest_at)
    ]).astype(jnp.int32)
    back_table = jnp.stack([chip_ids ^ chip, jnp.full((chips,), 1, jnp.int32) - core])
    near = core_ids[None, :] == core
    whole_table = jnp.stack([
        jnp.where(near, (chip_ids ^ chip)[:, None], chips).reshape(-1),
        jnp.where(near, core, chip_ids[:, None]).reshape(-1),
    ]).astype(jnp.int32)

    def spread(block):
        slices = block.reshape(dp_count, few, -1)
        return lax.all_to_all(slices, "dp", split_axis=0, concat_axis=0, tiled=True)

    def by_distance(values, at):
        ids = jnp.arange(values.shape[0], dtype=jnp.int32)
        hit = (ids[:, None] ^ ids[None, :]) == at
        hit = hit.reshape(hit.shape + (1,) * (values.ndim - 1))
        return jnp.sum(jnp.where(hit, values[None], 0), axis=1)

    def with_shares(block, shares):
        shares = shares.reshape(dp_count, -1)
        shares = jnp.pad(shares, ((0, 0), (0, -shares.shape[1] % HEAD)))
        slices = block.reshape(dp_count, few, -1)
        return beside(slices, shares.reshape(dp_count, -1, HEAD)).reshape(rows, -1)

    def shares_of(spread_rows, count):
        used = -(-count // HEAD)
        parts = spread_rows[:, : 3 * used, -HEAD:].astype(F32)
        parts = jnp.sum(jnp.sum(parts, axis=0).reshape(3, used * HEAD), axis=0)
        return parts[:count].reshape(seq_count, -1)

    def summed_seq(shares):
        shares = by_distance(shares, seq_at)
        pairs = [[(i, i ^ m) for i in range(seq_count)] for m in range(seq_count)]
        return sum(
            [lax.ppermute(shares[m], "seq", pairs[m]) for m in range(1, seq_count)], shares[0]
        )

    def to_other_side(value):
        return lax.ppermute(value, "seq", swap)

    def first_sent(sources, wide, send_table=send_table):
        return moved(
            send_table[:, :always], (always,), [sources], flops=SWAP_FLOPS, widths=[wide]
        )[0]

    def rest(widths, count, chunks):
        sent = [
            moved(send_table[:, always:], (count,), [chunk], widths=[wide])[0]
            for chunk, wide in zip(chunks, widths)
            if count
        ]
        return padded(always, [(few, wide) for wide in widths], [to_other_side(x) for x in sent])

    def the_rest(chunks, widths, *earlier):
        return lax.switch(
            after(level, *earlier), [partial(rest, widths, n) for n in levels], chunks
        )

    def place_rows(*groups, flops=1):
        first, *leaving = moved(place_table, (2,) * chips, *groups, far=1, flops=flops)
        return [first] + [to_chip(x, m + 1) for m, x in enumerate(leaving)]

    kind = lax.dynamic_slice(half_kind, (dp_at, seq_at // span), (1, 1))[0, 0]
    seen = jnp.where(kind == 0, piece, piece % (span // 2))
    at = seen.reshape(1).astype(jnp.int32)
    def earlier_kv(source, first, count):
        cols = slice(first * HEAD, (first + count) * HEAD)
        own = [source[:, q_width + a : q_width + a + kv_width][:, cols] for a in (0, kv_width)]
        own = jnp.stack(own)
        pieces = [lax.ppermute(own, "seq", later(d))[None] for d in range(1, span)]
        return pieces[0] if span == 2 else jnp.concatenate(pieces), own

    kv_first, own_first = earlier_kv(projections, 0, parts[0])
    kv_rest, _ = earlier_kv(after(projections, own_first), parts[0], kv_heads - parts[0])

    def back_to_owners(off):
        return [
            lax.ppermute(off[d - 1], "seq", [(b, a) for a, b in later(d)]) for d in range(1, span)
        ]

    def part_grads(part, at):
        first = sum(parts[:part])
        grad_query, own, q_sum, v_sum, off = attention(
            at,
            projections,
            grad_out,
            bias,
            kv_rest if part else kv_first,
            first - parts[0] if part else 0,
            first,
            parts[part],
            q_width,
            vmem=12 if part else 56,
        )
        return grad_query, own, off, (q_sum, v_sum)

    grad_query, own, off, sums = part_grads(0, after(at, send_table, place_table, whole_table))
    owns, parcels, all_sums = [own], [back_to_owners(off)], [sums]
    widths = [grad_query.shape[1]]
    chunks = [spread(after(grad_query, kv_rest))]
    grad_query, own, off, sums = part_grads(1, after(at, grad_query))
    sent = first_sent(after(chunks[0], own, parcels[0]), widths[0])
    owns.append(own)
    parcels.append(back_to_owners(off))
    all_sums.append(sums)
    crossed = [to_other_side(sent)]
    widths.append(grad_query.shape[1])
    terms = [jnp.concatenate([x[i] for x in all_sums], axis=1).reshape(devices, -1) for i in (0, 1)]
    terms = jnp.concatenate(terms, axis=1)
    chunks.append(spread(with_shares(grad_query, after(terms, sent))))
    terms = shares_of(chunks[1], terms.size // dp_count)
    parcel = [jnp.concatenate(x, axis=-1).astype(F32) for x in zip(*parcels)]
    own = jnp.concatenate(after(owns, sent), axis=-1)
    own = sum(parcel, own).astype(BF16)
    last = jnp.concatenate([own[0], own[1]], axis=1)
    widths.append(last.shape[1])
    sent = first_sent(after(chunks[1], terms), widths[1], gate(send_table, crossed[0], last))
    crossed.append(to_other_side(sent))
    chunks.append(spread(after(last, sent)))
    terms = summed_seq(after(terms, sent)) * factor
    more = the_rest(chunks[:2], widths[:2], sent)
    sent = first_sent(after(chunks[2], crossed[1], terms, more), widths[2])
    crossed.append(to_other_side(sent))
    groups = [list(group) for group in zip(chunks, crossed, more)]
    held = place_rows(*after(groups, sent))
    (more_last,) = the_rest(chunks[2:], widths[2:], held[0])
    held_last = place_rows([chunks[2], crossed[2], more_last], flops=PLACE_FLOPS)
    held = after(held, held_last[0])
    pieces, start = [], 0
    for group in groups:
        wide = group[-1].shape[-1]
        (returned,) = moved(back_table, (chips,), held, start=start, widths=[wide])
        pieces.append((held + [to_core(returned)], start))
        start += wide
    (returned,) = moved(back_table, (chips,), held_last)
    pieces.append((held_last + [to_core(returned)], 0))
    whole = joined(whole_table, pieces)
    return (
        whole.reshape(rows, width),
        terms[: q_width // devices],
        terms[q_width // devices :],
    )


def solution(mesh):
    in_specs = (P(("dp", "seq"), None), P(("dp", "seq"), None), P(), P(), P())
    out_specs = (P(("dp", "seq"), None), P(("dp", "seq")), P(("dp", "seq")))
    return jax.shard_map(local, mesh=mesh, in_specs=in_specs, out_specs=out_specs, check_vma=False)
```

```python
import math
from functools import partial, reduce

import jax
import jax.numpy as jnp
from jax import lax
from jax.experimental import pallas as pl
from jax.experimental.pallas import tpu as pltpu
from jax.sharding import PartitionSpec as P

HEAD = 128
NEG = -1e30
SWAP_FLOPS = 10**10
GATE_FLOPS = 6 * 10**9
PLACE_FLOPS = 17 * 10**8
F32 = jnp.float32
BF16 = jnp.bfloat16
SCALE = 1.0 / math.sqrt(HEAD)
LOG2_E = math.log2(math.e)


def dot(a, b, a_dim, b_dim):
    return lax.dot_general(a, b, (((a_dim,), (b_dim,)), ((), ())), preferred_element_type=F32)


def attention_kernel(
    group_size, earlier, at_ref, q_ref, k_ref, v_ref, grad_ref, bias_ref, *refs
):
    kv_off_ref = refs[0] if earlier else None
    outs = refs[1:] if earlier else refs
    dq_ref, dkv_ref, q_sum_ref, v_sum_ref = outs[:4]
    off_ref = outs[4] if earlier else None
    rows = q_ref.shape[0]

    keys = [k_ref[...]] + [kv_off_ref[d, 0] for d in range(earlier)]
    values = [v_ref[...]] + [kv_off_ref[d, 1] for d in range(earlier)]
    key_at = lax.broadcasted_iota(jnp.int32, (rows, rows), 0)
    query_at = lax.broadcasted_iota(jnp.int32, (rows, rows), 1)
    allowed = [key_at <= query_at] + [at_ref[0] > d for d in range(earlier)]

    def one_head(head, sums):
        grad_keys, grad_values = sums
        cols = slice(head * HEAD, (head + 1) * HEAD)
        query = (q_ref[:, cols].astype(F32) + bias_ref[:, cols].astype(F32)).astype(BF16)
        grad = grad_ref[:, cols]
        scores = [jnp.where(ok, dot(key, query, 1, 1), NEG) for ok, key in zip(allowed, keys)]
        tops = [jnp.max(s, axis=0, keepdims=True) for s in scores]
        top = reduce(jnp.maximum, tops)
        exps = [jnp.exp2((s - top) * (SCALE * LOG2_E)) for s in scores]
        grad_probs = [dot(value, grad, 1, 1) for value in values]
        total = sum(jnp.sum(e, axis=0, keepdims=True) for e in exps)
        mixed = sum(jnp.sum(e * g, axis=0, keepdims=True) for e, g in zip(exps, grad_probs))
        inverse = 1.0 / total
        delta = mixed * inverse
        scaled = inverse * SCALE
        weights = [(e * inverse).astype(BF16) for e in exps]
        grad_scores = [(e * scaled * (g - delta)).astype(BF16) for e, g in zip(exps, grad_probs)]
        grad_values = [t + dot(w, grad, 1, 0) for t, w in zip(grad_values, weights)]
        grad_keys = [t + dot(s, query, 1, 0) for t, s in zip(grad_keys, grad_scores)]
        grad_query = sum(dot(s, key, 0, 0) for s, key in zip(grad_scores, keys))
        dq_ref[:, cols] = grad_query.astype(BF16)
        q_sum_ref[:, cols] = jnp.sum(grad_query, axis=0, keepdims=True)
        return grad_keys, grad_values

    zeros = [jnp.zeros((rows, HEAD), F32) for _ in keys]
    sums = (zeros, zeros)
    for head in range(group_size):
        sums = one_head(head, sums)
    grad_keys, grad_values = sums
    dkv_ref[0] = grad_keys[0]
    dkv_ref[1] = grad_values[0]
    v_sum_ref[...] = sum(jnp.sum(g, axis=0, keepdims=True) for g in grad_values)
    for d in range(earlier):
        off_ref[d, 0] = grad_keys[d + 1].astype(BF16)
        off_ref[d, 1] = grad_values[d + 1].astype(BF16)


def attention(at, projections, grad_out, bias, kv_off, skip, first, groups, q_width, vmem):
    rows, width = projections.shape
    kv_width = (width - q_width) // 2
    group_size = q_width // kv_width
    earlier = kv_off.shape[0]
    wide = group_size * HEAD
    k_at = q_width // HEAD + first
    v_at = k_at + kv_width // HEAD
    in_specs = [
        pl.BlockSpec((rows, wide), lambda g, s: (0, first + g)),
        pl.BlockSpec((rows, HEAD), lambda g, s: (0, k_at + g)),
        pl.BlockSpec((rows, HEAD), lambda g, s: (0, v_at + g)),
        pl.BlockSpec((rows, wide), lambda g, s: (0, first + g)),
        pl.BlockSpec((1, wide), lambda g, s: (0, first + g)),
    ]
    operands = [projections, projections, projections, grad_out, bias]
    if earlier:
        in_specs.append(
            pl.BlockSpec((earlier, 2, rows, HEAD), lambda g, s: (0, 0, 0, skip + g))
        )
        operands.append(kv_off)
    out_specs = [
        pl.BlockSpec((rows, wide), lambda g, s: (0, g)),
        pl.BlockSpec((2, rows, HEAD), lambda g, s: (0, 0, g)),
        pl.BlockSpec((1, wide), lambda g, s: (0, g)),
        pl.BlockSpec((1, HEAD), lambda g, s: (0, g)),
    ]
    out_shape = [
        jax.ShapeDtypeStruct((rows, groups * wide), BF16),
        jax.ShapeDtypeStruct((2, rows, groups * HEAD), F32),
        jax.ShapeDtypeStruct((1, groups * wide), F32),
        jax.ShapeDtypeStruct((1, groups * HEAD), F32),
    ]
    if earlier:
        out_specs.append(pl.BlockSpec((earlier, 2, rows, HEAD), lambda g, s: (0, 0, 0, g)))
        out_shape.append(jax.ShapeDtypeStruct((earlier, 2, rows, groups * HEAD), BF16))
    flops = 10 * groups * group_size * rows * rows * HEAD * (1 + earlier)
    outs = pl.pallas_call(
        partial(attention_kernel, group_size, earlier),
        grid_spec=pltpu.PrefetchScalarGridSpec(
            num_scalar_prefetch=1, grid=(groups,), in_specs=in_specs, out_specs=out_specs
        ),
        out_shape=out_shape,
        compiler_params=pltpu.CompilerParams(vmem_limit_bytes=vmem * 1024 * 1024),
        cost_estimate=pl.CostEstimate(
            flops=flops,
            bytes_accessed=4 * rows * groups * wide,
            transcendentals=groups * group_size * rows * rows * (1 + earlier),
        ),
        name="attention_grads",
    )(at, *operands)
    return outs if earlier else (*outs, None)


def move_kernel(shape, widths, far, start, places_ref, *refs):
    *refs, sem = refs
    sources, outs = refs[: len(refs) - len(shape)], refs[len(refs) - len(shape) :]
    each = len(sources) // len(widths)
    first = 0
    for out_ref, count in zip(outs, shape):

        def fill(j, _, out_ref=out_ref, first=first):
            for at in range(each):

                @pl.when(places_ref[0, first + j] == at)
                def _():
                    column = 0
                    for source, wide in zip(sources[at::each], widths):
                        cols, taken = pl.ds(column, wide), pl.ds(start, wide)
                        index = places_ref[1, first + j]
                        if at < each - far:
                            out_ref[j, :, cols] = source[index, :, taken]
                        else:
                            copy = pltpu.make_async_copy(
                                source.at[index, :, taken], out_ref.at[j, :, cols], sem
                            )
                            copy.start()
                            copy.wait()
                        column += wide

            return 0

        lax.fori_loop(0, count, fill, 0)
        first += count


def moved(places, shape, *groups, far=0, flops=1, start=0, widths=None):
    vmem = pl.BlockSpec(memory_space=pltpu.VMEM)
    where = [vmem] * (len(groups[0]) - far) + [pl.BlockSpec(memory_space=pl.ANY)] * far
    rows = groups[0][0].shape[1]
    widths = widths or [sources[-1].shape[2] for sources in groups]
    width = sum(widths)
    return pl.pallas_call(
        partial(move_kernel, shape, widths, far, start),
        in_specs=[pl.BlockSpec(memory_space=pltpu.SMEM)] + where * len(groups),
        out_specs=[vmem for _ in shape],
        out_shape=[jax.ShapeDtypeStruct((n, rows, width), BF16) for n in shape],
        scratch_shapes=[pltpu.SemaphoreType.DMA],
        compiler_params=pltpu.CompilerParams(vmem_limit_bytes=10 * 1024 * 1024),
        cost_estimate=pl.CostEstimate(flops=flops, bytes_accessed=1, transcendentals=0),
        name="move_slices",
    )(places, *[source for sources in groups for source in sources])


def pad_kernel(*refs):
    for got_ref, out_ref in zip(refs[: len(refs) // 2], refs[len(refs) // 2 :]):
        out_ref[: got_ref.shape[0]] = got_ref[...]


def padded(size, shapes, gots):
    vmem = pl.BlockSpec(memory_space=pltpu.VMEM)
    return pl.pallas_call(
        pad_kernel if gots else lambda *outs: None,
        in_specs=[vmem for _ in gots],
        out_specs=[vmem if gots else pl.BlockSpec(memory_space=pl.ANY) for _ in shapes],
        out_shape=[jax.ShapeDtypeStruct((size, *shape), BF16) for shape in shapes],
        compiler_params=pltpu.CompilerParams(vmem_limit_bytes=10 * 1024 * 1024),
        name="pad_slices",
    )(*gots)


def join_kernel(parts, places_ref, *refs):
    sources, out_ref, sem = refs[:-2], refs[-2], refs[-1]
    each = len(sources) // len(parts)
    count = out_ref.shape[0]
    for wait in (False, True):
        column = 0
        for chunk, (wide, start) in enumerate(parts):
            for i in range(count):
                to = out_ref.at[i, :, pl.ds(column, wide)]
                done = sem.at[chunk * count + i]
                if wait:
                    pltpu.make_async_copy(to, to, done).wait()
                    continue
                for at, source in enumerate(sources[chunk * each : (chunk + 1) * each]):
                    taken = pl.ds(start if at < each - 1 else 0, wide)

                    @pl.when(places_ref[0, i] == at)
                    def _():
                        pltpu.make_async_copy(
                            source.at[places_ref[1, i], :, taken], to, done
                        ).start()

            column += wide


def joined(places, chunks):
    count, rows = places.shape[1], chunks[0][0][0].shape[1]
    parts = [(sources[-1].shape[-1], start) for sources, start in chunks]
    vmem = pl.BlockSpec(memory_space=pltpu.VMEM)
    operands = [x for sources, _ in chunks for x in sources]
    return pl.pallas_call(
        partial(join_kernel, parts),
        in_specs=[pl.BlockSpec(memory_space=pltpu.SMEM)] + [vmem for _ in operands],
        out_specs=pl.BlockSpec(memory_space=pl.ANY),
        out_shape=jax.ShapeDtypeStruct((count, rows, sum(wide for wide, _ in parts)), BF16),
        scratch_shapes=[pltpu.SemaphoreType.DMA((count * len(parts),))],
        compiler_params=pltpu.CompilerParams(vmem_limit_bytes=10 * 1024 * 1024),
        cost_estimate=pl.CostEstimate(flops=1, bytes_accessed=1, transcendentals=0),
        name="join_chunks",
    )(places, *operands)


def beside_kernel(block_ref, values_ref, out_ref):
    wide, count = block_ref.shape[-1], values_ref.shape[1]
    out_ref[:, :, :wide] = block_ref[...]
    out_ref[:, :, wide:] = jnp.zeros((*block_ref.shape[:2], HEAD), BF16)
    rest = values_ref[...]
    for part in range(3):
        piece = rest.astype(BF16)
        out_ref[:, part * count : (part + 1) * count, wide:] = piece
        rest = rest - piece.astype(F32)


def beside(block, values):
    vmem = pl.BlockSpec(memory_space=pltpu.VMEM)
    return pl.pallas_call(
        beside_kernel,
        in_specs=[vmem, vmem],
        out_specs=vmem,
        out_shape=jax.ShapeDtypeStruct((*block.shape[:2], block.shape[2] + HEAD), BF16),
        compiler_params=pltpu.CompilerParams(vmem_limit_bytes=10 * 1024 * 1024),
        cost_estimate=pl.CostEstimate(flops=GATE_FLOPS, bytes_accessed=1, transcendentals=0),
        name="beside",
    )(block, values)


def plan(dest_half, seq_count):
    windows = dest_half.shape[0]
    ids = jnp.arange(windows, dtype=jnp.int32)
    side = lax.axis_index("seq") // (seq_count // 2)
    crosses = (dest_half % 2) != jnp.arange(2, dtype=jnp.int32)[None, :]
    rank = jnp.sum(
        jnp.where((ids[None, :] < ids[:, None])[:, :, None], crosses[None, :, :], False), axis=1
    ).astype(jnp.int32)
    mine = jnp.arange(2, dtype=jnp.int32) == side
    cross_here = jnp.any(crosses & mine[None, :], axis=1)
    rank_here = jnp.sum(jnp.where(mine[None, :], rank, 0), axis=1)
    sent = jnp.sum(
        jnp.where((rank_here[None, :] == ids[:, None]) & cross_here[None, :], ids[None, :], 0),
        axis=1,
    )
    hit = dest_half[None, :, :] == (2 * ids + side)[:, None, None]
    from_other = jnp.any(hit & crosses[None], axis=(1, 2))
    place = jnp.sum(
        jnp.where(hit, jnp.where(crosses, rank, ids[:, None])[None], 0), axis=(1, 2)
    )
    return sent, from_other, place


def after(value, *earlier):
    return lax.optimization_barrier((value, earlier))[0]


def gate_kernel(in_ref, out_ref):
    out_ref[...] = in_ref[...]


def gate(value, *earlier):
    return pl.pallas_call(
        gate_kernel,
        out_shape=jax.ShapeDtypeStruct(value.shape, value.dtype),
        cost_estimate=pl.CostEstimate(flops=GATE_FLOPS, bytes_accessed=1, transcendentals=0),
        name="gate",
    )(after(value, *earlier))


def local(projections, grad_out, bias_q, half_kind, dest_half):
    dp_count = lax.axis_size("dp")
    seq_count = lax.axis_size("seq")
    dp_at = lax.axis_index("dp")
    seq_at = lax.axis_index("seq")
    rows, width = projections.shape
    q_width = bias_q.shape[0]
    kv_width = (width - q_width) // 2
    kv_heads = kv_width // HEAD
    span = seq_count // 2
    piece = seq_at % span
    bias = bias_q.reshape(1, q_width)
    factor = 1.0 / math.sqrt(rows * dp_count * seq_count)
    devices = dp_count * seq_count
    parts = [kv_heads // 2, kv_heads - kv_heads // 2]
    chips = dp_count // 2
    few = rows // dp_count
    chip, core = dp_at // 2, dp_at % 2
    chip_ids = jnp.arange(chips, dtype=jnp.int32)
    core_ids = jnp.arange(2, dtype=jnp.int32)
    swap = [(i, (i + span) % seq_count) for i in range(seq_count)]

    def later(by):
        return [(i, i + by) for i in range(seq_count) if i // span == (i + by) // span]

    def to_core(value):
        return lax.ppermute(value, "dp", [(i, i ^ 1) for i in range(dp_count)])

    def to_chip(value, by):
        return lax.ppermute(value, "dp", [(i, i ^ (2 * by)) for i in range(dp_count)])

    always = dp_count // 2
    sent_windows, from_other, place = plan(dest_half, seq_count)
    crossing = jnp.sum(dest_half[:, 0] % 2)
    step = max(1, always // 4)
    levels = list(range(0, always + 1, step))
    level = jnp.maximum(crossing - always + step - 1, 0) // step

    send_table = jnp.stack([jnp.zeros_like(sent_windows), sent_windows])
    dest_from = jnp.where(from_other, 1 + place // always, 0)
    dest_at = jnp.where(from_other, place % always, place)
    by_chip = chip_ids[:, None] ^ chip == chip_ids[None, :]
    place_table = jnp.stack([
        jnp.sum(jnp.where(by_chip[:, :, None], t.reshape(1, chips, 2), 0), axis=1).reshape(-1)
        for t in (dest_from, dest_at)
    ]).astype(jnp.int32)
    back_table = jnp.stack([chip_ids ^ chip, jnp.full((chips,), 1, jnp.int32) - core])
    near = core_ids[None, :] == core
    whole_table = jnp.stack([
        jnp.where(near, (chip_ids ^ chip)[:, None], chips).reshape(-1),
        jnp.where(near, core, chip_ids[:, None]).reshape(-1),
    ]).astype(jnp.int32)

    def spread(block):
        slices = block.reshape(dp_count, few, -1)
        return lax.all_to_all(slices, "dp", split_axis=0, concat_axis=0, tiled=True)

    def by_distance(values, at):
        ids = jnp.arange(values.shape[0], dtype=jnp.int32)
        hit = (ids[:, None] ^ ids[None, :]) == at
        hit = hit.reshape(hit.shape + (1,) * (values.ndim - 1))
        return jnp.sum(jnp.where(hit, values[None], 0), axis=1)

    def with_shares(block, shares):
        shares = shares.reshape(dp_count, -1)
        shares = jnp.pad(shares, ((0, 0), (0, -shares.shape[1] % HEAD)))
        slices = block.reshape(dp_count, few, -1)
        return beside(slices, shares.reshape(dp_count, -1, HEAD)).reshape(rows, -1)

    def shares_of(spread_rows, count):
        used = -(-count // HEAD)
        parts = spread_rows[:, : 3 * used, -HEAD:].astype(F32)
        parts = jnp.sum(jnp.sum(parts, axis=0).reshape(3, used * HEAD), axis=0)
        return parts[:count].reshape(seq_count, -1)

    def summed_seq(shares):
        shares = by_distance(shares, seq_at)
        pairs = [[(i, i ^ m) for i in range(seq_count)] for m in range(seq_count)]
        return sum(
            [lax.ppermute(shares[m], "seq", pairs[m]) for m in range(1, seq_count)], shares[0]
        )

    def to_other_side(value):
        return lax.ppermute(value, "seq", swap)

    first_table = send_table[:, :always]

    def first_sent(sources, wide, table=first_table):
        return moved(table, (always,), [sources], flops=SWAP_FLOPS, widths=[wide])[0]

    def rest(widths, count, chunks):
        sent = [
            moved(send_table[:, always:], (count,), [chunk], widths=[wide])[0]
            for chunk, wide in zip(chunks, widths)
            if count
        ]
        return padded(always, [(few, wide) for wide in widths], [to_other_side(x) for x in sent])

    def the_rest(chunks, widths, *earlier):
        return lax.switch(
            after(level, *earlier), [partial(rest, widths, n) for n in levels], chunks
        )

    def place_rows(*groups, flops=1):
        first, *leaving = moved(place_table, (2,) * chips, *groups, far=1, flops=flops)
        return [first] + [to_chip(x, m + 1) for m, x in enumerate(leaving)]

    kind = lax.dynamic_slice(half_kind, (dp_at, seq_at // span), (1, 1))[0, 0]
    seen = jnp.where(kind == 0, piece, piece % (span // 2))
    at = seen.reshape(1).astype(jnp.int32)
    def earlier_kv(source, first, count):
        cols = slice(first * HEAD, (first + count) * HEAD)
        own = [source[:, q_width + a : q_width + a + kv_width][:, cols] for a in (0, kv_width)]
        own = jnp.stack(own)
        pieces = [lax.ppermute(own, "seq", later(d))[None] for d in range(1, span)]
        return pieces[0] if span == 2 else jnp.concatenate(pieces), own

    kv_first, own_first = earlier_kv(projections, 0, parts[0])
    kv_rest, _ = earlier_kv(after(projections, own_first), parts[0], kv_heads - parts[0])

    def back_to_owners(off):
        return [
            lax.ppermute(off[d - 1], "seq", [(b, a) for a, b in later(d)]) for d in range(1, span)
        ]

    def part_grads(part, at):
        first = sum(parts[:part])
        grad_query, own, q_sum, v_sum, off = attention(
            at,
            projections,
            grad_out,
            bias,
            kv_rest if part else kv_first,
            first - parts[0] if part else 0,
            first,
            parts[part],
            q_width,
            vmem=56,
        )
        return grad_query, own, off, (q_sum, v_sum)

    grad_query, own, off, sums = part_grads(0, after(at, first_table, place_table, whole_table))
    owns, parcels, all_sums = [own], [back_to_owners(off)], [sums]
    widths = [grad_query.shape[1]]
    chunks = [spread(after(grad_query, kv_rest))]
    grad_query, own, off, sums = part_grads(1, after(at, grad_query))
    sent = first_sent(after(chunks[0], own, parcels[0]), widths[0])
    owns.append(own)
    parcels.append(back_to_owners(off))
    all_sums.append(sums)
    crossed = [to_other_side(sent)]
    widths.append(grad_query.shape[1])
    all_sums = after(all_sums, sent)
    terms = [jnp.concatenate([x[i] for x in all_sums], axis=1).reshape(devices, -1) for i in (0, 1)]
    terms = jnp.concatenate(terms, axis=1)
    chunks.append(spread(with_shares(grad_query, terms)))
    terms = shares_of(chunks[1], terms.size // dp_count)
    parcel = [jnp.concatenate(x, axis=-1).astype(F32) for x in zip(*parcels)]
    own = jnp.concatenate(after(owns, sent), axis=-1)
    own = sum(parcel, own).astype(BF16)
    last = jnp.concatenate([own[0], own[1]], axis=1)
    widths.append(last.shape[1])
    sent = first_sent(after(chunks[1], terms), widths[1], gate(first_table, crossed[0], last))
    crossed.append(to_other_side(sent))
    chunks.append(spread(after(last, sent)))
    terms = summed_seq(after(terms, sent)) * factor
    more = the_rest(chunks[:2], widths[:2], sent)
    sent = first_sent(after(chunks[2], crossed[1], terms, more), widths[2])
    crossed.append(to_other_side(sent))
    groups = [list(group) for group in zip(chunks, crossed, more)]
    held = place_rows(*after(groups, sent))
    (more_last,) = the_rest(chunks[2:], widths[2:], held[0])
    held_last = place_rows([chunks[2], crossed[2], more_last], flops=PLACE_FLOPS)
    held = after(held, held_last[0])
    pieces, start = [], 0
    for group in groups:
        wide = group[-1].shape[-1]
        (returned,) = moved(back_table, (chips,), held, start=start, widths=[wide])
        pieces.append((held + [to_core(returned)], start))
        start += wide
    (returned,) = moved(back_table, (chips,), held_last)
    pieces.append((held_last + [to_core(returned)], 0))
    whole = joined(whole_table, pieces)
    return (
        whole.reshape(rows, width),
        terms[: q_width // devices],
        terms[q_width // devices :],
    )


def solution(mesh):
    in_specs = (P(("dp", "seq"), None), P(("dp", "seq"), None), P(), P(), P())
    out_specs = (P(("dp", "seq"), None), P(("dp", "seq")), P(("dp", "seq")))
    return jax.shard_map(local, mesh=mesh, in_specs=in_specs, out_specs=out_specs, check_vma=False)
```

```python
import math
from functools import partial, reduce

import jax
import jax.numpy as jnp
from jax import lax
from jax.experimental import pallas as pl
from jax.experimental.pallas import tpu as pltpu
from jax.sharding import PartitionSpec as P

HEAD = 128
NEG = -1e30
SWAP_FLOPS = 10**10
GATE_FLOPS = 6 * 10**9
PLACE_FLOPS = 17 * 10**8
F32 = jnp.float32
BF16 = jnp.bfloat16
SCALE = 1.0 / math.sqrt(HEAD)
LOG2_E = math.log2(math.e)


def dot(a, b, a_dim, b_dim):
    return lax.dot_general(a, b, (((a_dim,), (b_dim,)), ((), ())), preferred_element_type=F32)


def attention_kernel(
    group_size, earlier, at_ref, q_ref, k_ref, v_ref, grad_ref, bias_ref, *refs
):
    kv_off_ref = refs[0] if earlier else None
    outs = refs[1:] if earlier else refs
    dq_ref, dkv_ref, q_sum_ref, v_sum_ref = outs[:4]
    off_ref = outs[4] if earlier else None
    rows = q_ref.shape[0]

    keys = [k_ref[...]] + [kv_off_ref[d, 0] for d in range(earlier)]
    values = [v_ref[...]] + [kv_off_ref[d, 1] for d in range(earlier)]
    key_at = lax.broadcasted_iota(jnp.int32, (rows, rows), 0)
    query_at = lax.broadcasted_iota(jnp.int32, (rows, rows), 1)
    allowed = [key_at <= query_at] + [at_ref[0] > d for d in range(earlier)]

    def one_head(head, sums):
        grad_keys, grad_values = sums
        cols = slice(head * HEAD, (head + 1) * HEAD)
        query = (q_ref[:, cols].astype(F32) + bias_ref[:, cols].astype(F32)).astype(BF16)
        grad = grad_ref[:, cols]
        scores = [jnp.where(ok, dot(key, query, 1, 1), NEG) for ok, key in zip(allowed, keys)]
        tops = [jnp.max(s, axis=0, keepdims=True) for s in scores]
        top = reduce(jnp.maximum, tops)
        exps = [jnp.exp2((s - top) * (SCALE * LOG2_E)) for s in scores]
        grad_probs = [dot(value, grad, 1, 1) for value in values]
        total = sum(jnp.sum(e, axis=0, keepdims=True) for e in exps)
        mixed = sum(jnp.sum(e * g, axis=0, keepdims=True) for e, g in zip(exps, grad_probs))
        inverse = 1.0 / total
        delta = mixed * inverse
        scaled = inverse * SCALE
        weights = [(e * inverse).astype(BF16) for e in exps]
        grad_scores = [(e * scaled * (g - delta)).astype(BF16) for e, g in zip(exps, grad_probs)]
        grad_values = [t + dot(w, grad, 1, 0) for t, w in zip(grad_values, weights)]
        grad_keys = [t + dot(s, query, 1, 0) for t, s in zip(grad_keys, grad_scores)]
        grad_query = sum(dot(s, key, 0, 0) for s, key in zip(grad_scores, keys))
        dq_ref[:, cols] = grad_query.astype(BF16)
        q_sum_ref[:, cols] = jnp.sum(grad_query, axis=0, keepdims=True)
        return grad_keys, grad_values

    zeros = [jnp.zeros((rows, HEAD), F32) for _ in keys]
    sums = (zeros, zeros)
    for head in range(group_size):
        sums = one_head(head, sums)
    grad_keys, grad_values = sums
    dkv_ref[0] = grad_keys[0]
    dkv_ref[1] = grad_values[0]
    v_sum_ref[...] = sum(jnp.sum(g, axis=0, keepdims=True) for g in grad_values)
    for d in range(earlier):
        off_ref[d, 0] = grad_keys[d + 1].astype(BF16)
        off_ref[d, 1] = grad_values[d + 1].astype(BF16)


def attention(at, projections, grad_out, bias, kv_off, skip, first, groups, q_width, vmem):
    rows, width = projections.shape
    kv_width = (width - q_width) // 2
    group_size = q_width // kv_width
    earlier = kv_off.shape[0]
    wide = group_size * HEAD
    k_at = q_width // HEAD + first
    v_at = k_at + kv_width // HEAD
    in_specs = [
        pl.BlockSpec((rows, wide), lambda g, s: (0, first + g)),
        pl.BlockSpec((rows, HEAD), lambda g, s: (0, k_at + g)),
        pl.BlockSpec((rows, HEAD), lambda g, s: (0, v_at + g)),
        pl.BlockSpec((rows, wide), lambda g, s: (0, first + g)),
        pl.BlockSpec((1, wide), lambda g, s: (0, first + g)),
    ]
    operands = [projections, projections, projections, grad_out, bias]
    if earlier:
        in_specs.append(
            pl.BlockSpec((earlier, 2, rows, HEAD), lambda g, s: (0, 0, 0, skip + g))
        )
        operands.append(kv_off)
    out_specs = [
        pl.BlockSpec((rows, wide), lambda g, s: (0, g)),
        pl.BlockSpec((2, rows, HEAD), lambda g, s: (0, 0, g)),
        pl.BlockSpec((1, wide), lambda g, s: (0, g)),
        pl.BlockSpec((1, HEAD), lambda g, s: (0, g)),
    ]
    out_shape = [
        jax.ShapeDtypeStruct((rows, groups * wide), BF16),
        jax.ShapeDtypeStruct((2, rows, groups * HEAD), F32),
        jax.ShapeDtypeStruct((1, groups * wide), F32),
        jax.ShapeDtypeStruct((1, groups * HEAD), F32),
    ]
    if earlier:
        out_specs.append(pl.BlockSpec((earlier, 2, rows, HEAD), lambda g, s: (0, 0, 0, g)))
        out_shape.append(jax.ShapeDtypeStruct((earlier, 2, rows, groups * HEAD), BF16))
    flops = 10 * groups * group_size * rows * rows * HEAD * (1 + earlier)
    outs = pl.pallas_call(
        partial(attention_kernel, group_size, earlier),
        grid_spec=pltpu.PrefetchScalarGridSpec(
            num_scalar_prefetch=1, grid=(groups,), in_specs=in_specs, out_specs=out_specs
        ),
        out_shape=out_shape,
        compiler_params=pltpu.CompilerParams(vmem_limit_bytes=vmem * 1024 * 1024),
        cost_estimate=pl.CostEstimate(
            flops=flops,
            bytes_accessed=4 * rows * groups * wide,
            transcendentals=groups * group_size * rows * rows * (1 + earlier),
        ),
        name="attention_grads",
    )(at, *operands)
    return outs if earlier else (*outs, None)


def move_kernel(shape, widths, far, start, places_ref, *refs):
    *refs, sem = refs
    sources, outs = refs[: len(refs) - len(shape)], refs[len(refs) - len(shape) :]
    each = len(sources) // len(widths)
    first = 0
    for out_ref, count in zip(outs, shape):

        def fill(j, _, out_ref=out_ref, first=first):
            for at in range(each):

                @pl.when(places_ref[0, first + j] == at)
                def _():
                    column = 0
                    for source, wide in zip(sources[at::each], widths):
                        cols, taken = pl.ds(column, wide), pl.ds(start, wide)
                        index = places_ref[1, first + j]
                        if at < each - far:
                            out_ref[j, :, cols] = source[index, :, taken]
                        else:
                            copy = pltpu.make_async_copy(
                                source.at[index, :, taken], out_ref.at[j, :, cols], sem
                            )
                            copy.start()
                            copy.wait()
                        column += wide

            return 0

        lax.fori_loop(0, count, fill, 0)
        first += count


def moved(places, shape, *groups, far=0, flops=1, start=0, widths=None):
    vmem = pl.BlockSpec(memory_space=pltpu.VMEM)
    where = [vmem] * (len(groups[0]) - far) + [pl.BlockSpec(memory_space=pl.ANY)] * far
    rows = groups[0][0].shape[1]
    widths = widths or [sources[-1].shape[2] for sources in groups]
    width = sum(widths)
    return pl.pallas_call(
        partial(move_kernel, shape, widths, far, start),
        in_specs=[pl.BlockSpec(memory_space=pltpu.SMEM)] + where * len(groups),
        out_specs=[vmem for _ in shape],
        out_shape=[jax.ShapeDtypeStruct((n, rows, width), BF16) for n in shape],
        scratch_shapes=[pltpu.SemaphoreType.DMA],
        compiler_params=pltpu.CompilerParams(vmem_limit_bytes=10 * 1024 * 1024),
        cost_estimate=pl.CostEstimate(flops=flops, bytes_accessed=1, transcendentals=0),
        name="move_slices",
    )(places, *[source for sources in groups for source in sources])


def pad_kernel(*refs):
    for got_ref, out_ref in zip(refs[: len(refs) // 2], refs[len(refs) // 2 :]):
        out_ref[: got_ref.shape[0]] = got_ref[...]


def padded(size, shapes, gots):
    vmem = pl.BlockSpec(memory_space=pltpu.VMEM)
    return pl.pallas_call(
        pad_kernel if gots else lambda *outs: None,
        in_specs=[vmem for _ in gots],
        out_specs=[vmem if gots else pl.BlockSpec(memory_space=pl.ANY) for _ in shapes],
        out_shape=[jax.ShapeDtypeStruct((size, *shape), BF16) for shape in shapes],
        compiler_params=pltpu.CompilerParams(vmem_limit_bytes=10 * 1024 * 1024),
        name="pad_slices",
    )(*gots)


def join_kernel(parts, places_ref, *refs):
    sources, out_ref, sem = refs[:-2], refs[-2], refs[-1]
    each = len(sources) // len(parts)
    count = out_ref.shape[0]
    for wait in (False, True):
        column = 0
        for chunk, (wide, start) in enumerate(parts):
            for i in range(count):
                to = out_ref.at[i, :, pl.ds(column, wide)]
                done = sem.at[chunk * count + i]
                if wait:
                    pltpu.make_async_copy(to, to, done).wait()
                    continue
                for at, source in enumerate(sources[chunk * each : (chunk + 1) * each]):
                    taken = pl.ds(start if at < each - 1 else 0, wide)

                    @pl.when(places_ref[0, i] == at)
                    def _():
                        pltpu.make_async_copy(
                            source.at[places_ref[1, i], :, taken], to, done
                        ).start()

            column += wide


def joined(places, chunks):
    count, rows = places.shape[1], chunks[0][0][0].shape[1]
    parts = [(sources[-1].shape[-1], start) for sources, start in chunks]
    vmem = pl.BlockSpec(memory_space=pltpu.VMEM)
    operands = [x for sources, _ in chunks for x in sources]
    return pl.pallas_call(
        partial(join_kernel, parts),
        in_specs=[pl.BlockSpec(memory_space=pltpu.SMEM)] + [vmem for _ in operands],
        out_specs=pl.BlockSpec(memory_space=pl.ANY),
        out_shape=jax.ShapeDtypeStruct((count, rows, sum(wide for wide, _ in parts)), BF16),
        scratch_shapes=[pltpu.SemaphoreType.DMA((count * len(parts),))],
        compiler_params=pltpu.CompilerParams(vmem_limit_bytes=10 * 1024 * 1024),
        cost_estimate=pl.CostEstimate(flops=1, bytes_accessed=1, transcendentals=0),
        name="join_chunks",
    )(places, *operands)


def beside_kernel(block_ref, values_ref, out_ref):
    wide = block_ref.shape[-1]
    out_ref[:, :, :wide] = block_ref[...]
    rest, pieces = values_ref[...], []
    for _ in range(3):
        pieces.append(rest.astype(BF16).astype(F32))
        rest = rest - pieces[-1]
    slices, count, _ = rest.shape
    pieces.append(jnp.zeros((slices, out_ref.shape[1] - 3 * count, HEAD), F32))
    out_ref[:, :, wide:] = jnp.concatenate(pieces, axis=1).astype(BF16)


def beside(block, values):
    vmem = pl.BlockSpec(memory_space=pltpu.VMEM)
    return pl.pallas_call(
        beside_kernel,
        in_specs=[vmem, vmem],
        out_specs=vmem,
        out_shape=jax.ShapeDtypeStruct((*block.shape[:2], block.shape[2] + HEAD), BF16),
        compiler_params=pltpu.CompilerParams(vmem_limit_bytes=10 * 1024 * 1024),
        cost_estimate=pl.CostEstimate(flops=GATE_FLOPS, bytes_accessed=1, transcendentals=0),
        name="beside",
    )(block, values)


def plan(dest_half, seq_count):
    windows = dest_half.shape[0]
    ids = jnp.arange(windows, dtype=jnp.int32)
    side = lax.axis_index("seq") // (seq_count // 2)
    crosses = (dest_half % 2) != jnp.arange(2, dtype=jnp.int32)[None, :]
    rank = jnp.sum(
        jnp.where((ids[None, :] < ids[:, None])[:, :, None], crosses[None, :, :], False), axis=1
    ).astype(jnp.int32)
    mine = jnp.arange(2, dtype=jnp.int32) == side
    cross_here = jnp.any(crosses & mine[None, :], axis=1)
    rank_here = jnp.sum(jnp.where(mine[None, :], rank, 0), axis=1)
    sent = jnp.sum(
        jnp.where((rank_here[None, :] == ids[:, None]) & cross_here[None, :], ids[None, :], 0),
        axis=1,
    )
    hit = dest_half[None, :, :] == (2 * ids + side)[:, None, None]
    from_other = jnp.any(hit & crosses[None], axis=(1, 2))
    place = jnp.sum(
        jnp.where(hit, jnp.where(crosses, rank, ids[:, None])[None], 0), axis=(1, 2)
    )
    return sent, from_other, place


def after(value, *earlier):
    return lax.optimization_barrier((value, earlier))[0]


def gate_kernel(in_ref, out_ref):
    for i in range(in_ref.shape[0]):
        for j in range(in_ref.shape[1]):
            out_ref[i, j] = in_ref[i, j]


def gate(value, *earlier):
    smem = pl.BlockSpec(memory_space=pltpu.SMEM)
    return pl.pallas_call(
        gate_kernel,
        in_specs=[smem],
        out_specs=smem,
        out_shape=jax.ShapeDtypeStruct(value.shape, value.dtype),
        cost_estimate=pl.CostEstimate(flops=GATE_FLOPS, bytes_accessed=1, transcendentals=0),
        name="gate",
    )(after(value, *earlier))


def local(projections, grad_out, bias_q, half_kind, dest_half):
    dp_count = lax.axis_size("dp")
    seq_count = lax.axis_size("seq")
    dp_at = lax.axis_index("dp")
    seq_at = lax.axis_index("seq")
    rows, width = projections.shape
    q_width = bias_q.shape[0]
    kv_width = (width - q_width) // 2
    kv_heads = kv_width // HEAD
    span = seq_count // 2
    piece = seq_at % span
    bias = bias_q.reshape(1, q_width)
    factor = 1.0 / math.sqrt(rows * dp_count * seq_count)
    devices = dp_count * seq_count
    parts = [kv_heads // 2, kv_heads - kv_heads // 2]
    chips = dp_count // 2
    few = rows // dp_count
    chip, core = dp_at // 2, dp_at % 2
    chip_ids = jnp.arange(chips, dtype=jnp.int32)
    core_ids = jnp.arange(2, dtype=jnp.int32)
    swap = [(i, (i + span) % seq_count) for i in range(seq_count)]

    def later(by):
        return [(i, i + by) for i in range(seq_count) if i // span == (i + by) // span]

    def to_core(value):
        return lax.ppermute(value, "dp", [(i, i ^ 1) for i in range(dp_count)])

    def to_chip(value, by):
        return lax.ppermute(value, "dp", [(i, i ^ (2 * by)) for i in range(dp_count)])

    always = dp_count // 2
    sent_windows, from_other, place = plan(dest_half, seq_count)
    crossing = jnp.sum(dest_half[:, 0] % 2)
    step = max(1, always // 4)
    levels = list(range(0, always + 1, step))
    level = jnp.maximum(crossing - always + step - 1, 0) // step

    send_table = jnp.stack([jnp.zeros_like(sent_windows), sent_windows])
    dest_from = jnp.where(from_other, 1 + place // always, 0)
    dest_at = jnp.where(from_other, place % always, place)
    by_chip = chip_ids[:, None] ^ chip == chip_ids[None, :]
    place_table = jnp.stack([
        jnp.sum(jnp.where(by_chip[:, :, None], t.reshape(1, chips, 2), 0), axis=1).reshape(-1)
        for t in (dest_from, dest_at)
    ]).astype(jnp.int32)
    back_table = jnp.stack([chip_ids ^ chip, jnp.full((chips,), 1, jnp.int32) - core])
    near = core_ids[None, :] == core
    whole_table = jnp.stack([
        jnp.where(near, (chip_ids ^ chip)[:, None], chips).reshape(-1),
        jnp.where(near, core, chip_ids[:, None]).reshape(-1),
    ]).astype(jnp.int32)

    def spread(block):
        slices = block.reshape(dp_count, few, -1)
        return lax.all_to_all(slices, "dp", split_axis=0, concat_axis=0, tiled=True)

    def by_distance(values, at):
        ids = jnp.arange(values.shape[0], dtype=jnp.int32)
        hit = (ids[:, None] ^ ids[None, :]) == at
        hit = hit.reshape(hit.shape + (1,) * (values.ndim - 1))
        return jnp.sum(jnp.where(hit, values[None], 0), axis=1)

    def with_shares(block, shares):
        shares = shares.reshape(dp_count, -1)
        shares = jnp.pad(shares, ((0, 0), (0, -shares.shape[1] % HEAD)))
        slices = block.reshape(dp_count, few, -1)
        return beside(slices, shares.reshape(dp_count, -1, HEAD)).reshape(rows, -1)

    def shares_of(spread_rows, count):
        used = -(-count // HEAD)
        parts = spread_rows[:, : 3 * used, -HEAD:].astype(F32)
        parts = jnp.sum(jnp.sum(parts, axis=0).reshape(3, used * HEAD), axis=0)
        return parts[:count].reshape(seq_count, -1)

    def summed_seq(shares):
        shares = by_distance(shares, seq_at)
        pairs = [[(i, i ^ m) for i in range(seq_count)] for m in range(seq_count)]
        return sum(
            [lax.ppermute(shares[m], "seq", pairs[m]) for m in range(1, seq_count)], shares[0]
        )

    def to_other_side(value):
        return lax.ppermute(value, "seq", swap)

    first_table = send_table[:, :always]

    def first_sent(sources, wide, table=first_table):
        return moved(table, (always,), [sources], flops=SWAP_FLOPS, widths=[wide])[0]

    def rest(widths, count, chunks):
        sent = [
            moved(send_table[:, always:], (count,), [chunk], widths=[wide])[0]
            for chunk, wide in zip(chunks, widths)
            if count
        ]
        return padded(always, [(few, wide) for wide in widths], [to_other_side(x) for x in sent])

    def the_rest(chunks, widths, *earlier):
        return lax.switch(
            after(level, *earlier), [partial(rest, widths, n) for n in levels], chunks
        )

    def place_rows(*groups, flops=1):
        first, *leaving = moved(place_table, (2,) * chips, *groups, far=1, flops=flops)
        return [first] + [to_chip(x, m + 1) for m, x in enumerate(leaving)]

    kind = lax.dynamic_slice(half_kind, (dp_at, seq_at // span), (1, 1))[0, 0]
    seen = jnp.where(kind == 0, piece, piece % (span // 2))
    at = seen.reshape(1).astype(jnp.int32)
    def earlier_kv(source, first, count):
        cols = slice(first * HEAD, (first + count) * HEAD)
        own = [source[:, q_width + a : q_width + a + kv_width][:, cols] for a in (0, kv_width)]
        own = jnp.stack(own)
        pieces = [lax.ppermute(own, "seq", later(d))[None] for d in range(1, span)]
        return pieces[0] if span == 2 else jnp.concatenate(pieces), own

    kv_first, own_first = earlier_kv(projections, 0, parts[0])
    kv_rest, _ = earlier_kv(after(projections, own_first), parts[0], kv_heads - parts[0])

    def back_to_owners(off):
        return [
            lax.ppermute(off[d - 1], "seq", [(b, a) for a, b in later(d)]) for d in range(1, span)
        ]

    def part_grads(part, at):
        first = sum(parts[:part])
        grad_query, own, q_sum, v_sum, off = attention(
            at,
            projections,
            grad_out,
            bias,
            kv_rest if part else kv_first,
            first - parts[0] if part else 0,
            first,
            parts[part],
            q_width,
            vmem=56,
        )
        return grad_query, own, off, (q_sum, v_sum)

    grad_query, own, off, sums = part_grads(0, after(at, first_table, place_table, whole_table))
    owns, parcels, all_sums = [own], [back_to_owners(off)], [sums]
    widths = [grad_query.shape[1]]
    chunks = [spread(after(grad_query, kv_rest))]
    grad_query, own, off, sums = part_grads(1, after(at, grad_query))
    sent = first_sent(after(chunks[0], own, parcels[0]), widths[0])
    owns.append(own)
    parcels.append(back_to_owners(off))
    all_sums.append(sums)
    crossed = [to_other_side(sent)]
    widths.append(grad_query.shape[1])
    all_sums = after(all_sums, sent)
    terms = [jnp.concatenate([x[i] for x in all_sums], axis=1).reshape(devices, -1) for i in (0, 1)]
    terms = jnp.concatenate(terms, axis=1)
    chunks.append(spread(with_shares(grad_query, terms)))
    terms = shares_of(chunks[1], terms.size // dp_count)
    parcel = [jnp.concatenate(x, axis=-1).astype(F32) for x in zip(*parcels)]
    own = jnp.concatenate(after(owns, sent), axis=-1)
    own = sum(parcel, own).astype(BF16)
    last = jnp.concatenate([own[0], own[1]], axis=1)
    widths.append(last.shape[1])
    sent = first_sent(after(chunks[1], terms), widths[1], gate(first_table, crossed[0], last))
    crossed.append(to_other_side(sent))
    chunks.append(spread(after(last, sent)))
    terms = summed_seq(after(terms, sent)) * factor
    more = the_rest(chunks[:2], widths[:2], sent)
    sent = first_sent(after(chunks[2], crossed[1], terms, more), widths[2])
    crossed.append(to_other_side(sent))
    groups = [list(group) for group in zip(chunks, crossed, more)]
    held = place_rows(*after(groups, sent))
    (more_last,) = the_rest(chunks[2:], widths[2:], held[0])
    bias_grad, value_bias_grad = terms[: q_width // devices], terms[q_width // devices :]
    last = after([chunks[2], crossed[2], more_last], bias_grad, value_bias_grad)
    held_last = place_rows(last, flops=PLACE_FLOPS)
    held = after(held, held_last[0])
    pieces, start = [], 0
    for group in groups:
        wide = group[-1].shape[-1]
        (returned,) = moved(back_table, (chips,), held, start=start, widths=[wide])
        pieces.append((held + [to_core(returned)], start))
        start += wide
    (returned,) = moved(back_table, (chips,), held_last)
    pieces.append((held_last + [to_core(returned)], 0))
    whole = joined(whole_table, pieces)
    return whole.reshape(rows, width), bias_grad, value_bias_grad


def solution(mesh):
    in_specs = (P(("dp", "seq"), None), P(("dp", "seq"), None), P(), P(), P())
    out_specs = (P(("dp", "seq"), None), P(("dp", "seq")), P(("dp", "seq")))
    return jax.shard_map(local, mesh=mesh, in_specs=in_specs, out_specs=out_specs, check_vma=False)
```
